128 devices in a mesh: edge: 4 (over x), cols: 32 (over z, y, core).
Axes of the slice: x: 4, y: 4, z: 4, core: 2. Of those that a mesh axis runs over, the one named last changes fastest.
Arguments:
- atmos_state: bfloat16 [11, 128, 16, 4096], P(None, None, 'edge', 'cols'), may hold values from -5 to 6
- horiz_wind: float32 [2, 128, 16, 4096], P(None, None, 'edge', 'cols'), may hold values from -6 to 6
- route_map: int32 [16, 4096], P('edge', 'cols'), may hold values from 0 to 31, as said below
- diffusivity: float32 [128, 131072], P(None, ('edge', 'cols')), may hold values from 0.1 to 100
- branch_mask: int32 [128, 131072], P(None, ('edge', 'cols')), may hold values from 0 to 3
- phys_state: float32 [8, 128, 131072], P(None, None, ('edge', 'cols')), may hold values from -6 to 6
Outputs:
- new_state: bfloat16 [11, 128, 16, 4096], P(None, None, 'edge', 'cols')
- phys_next: float32 [8, 128, 131072], P(None, None, ('edge', 'cols'))
The draws below stay inside these ranges and needn't reach their ends.
Inputs may be any that keep to these rules, and one draw needn't show every extreme that they name: `route_map`: on every device, at most 32 of its columns go to any one group, and exactly 32 go to one of them.
All inputs are finite; a program needn't handle non-finite values.
Results may differ from the reference program's by a relative error of at most 0.005.
Values may be sent and summed in bfloat16 or wider, within the bound.
A program may use at most 192 MiB of HBM per device.

```python
import math
import jax
import jax.numpy as jnp
import numpy as np
from jax import lax

FIELDS = 11
LEV = 128
NP = 4
PF = 8
NPASS = 2
X_DEV = 4
Y_DEV = 128
CAP = 32
SLOTS = 131072
NX = 16
NY = 4096
N_EDGE = 4
N_COLS = 32


def draw_route_map(key, part):
    key = jax.random.fold_in(key, 11)
    edge_count = NX // X_DEV
    col_count = NY // Y_DEV
    columns = X_DEV * Y_DEV
    capacity = 2 * columns // col_count
    device_keys = jax.random.split(key, edge_count * col_count + 1)
    ranks = jax.vmap(lambda one_key: jax.random.permutation(one_key, columns))(device_keys[1:])
    hottest = jax.random.randint(device_keys[0], (edge_count * col_count, 1), 0, col_count)
    others = (hottest + 1 + (ranks - capacity) % (col_count - 1)) % col_count
    chosen = jnp.where(ranks < capacity, hottest, others)
    grid_map = chosen.reshape(edge_count, col_count, X_DEV, Y_DEV)
    grid_map = jnp.moveaxis(grid_map, 1, 2)
    return grid_map.reshape(NX, NY).astype(jnp.int32)


def level_profile(amplitude):
    levels_at = jnp.arange(LEV, dtype=jnp.float32)
    shape_row = 0.7 + 0.3 * jnp.cos(math.pi * levels_at / LEV)
    return amplitude * shape_row[None, :]


def draw_atmos_state(key, part):
    key = jax.random.fold_in(key, 21)
    rough_key, amp_key = jax.random.split(key)
    rough = jnp.clip(jax.random.normal(rough_key, (FIELDS, LEV, NX, NY), jnp.float32), -5.0, 5.0)
    amplitude = jax.random.uniform(amp_key, (FIELDS, 1), jnp.float32, 0.5, 0.9)
    smooth = level_profile(amplitude)
    return (rough + smooth[:, :, None, None]).astype(jnp.bfloat16)


def draw_diffusivity(key, part):
    key = jax.random.fold_in(key, 23)
    base_key, pick_key, strong_key = jax.random.split(key, 3)
    base = jnp.exp(jax.random.uniform(base_key, (LEV, SLOTS), jnp.float32, math.log(0.1), math.log(10.0)))
    share = 0.125
    strong = jax.random.uniform(strong_key, (LEV, SLOTS), jnp.float32, 60.0, 100.0)
    picked = jax.random.uniform(pick_key, (1, SLOTS), jnp.float32) < share
    return jnp.where(picked, strong, base).astype(jnp.float32)


def touch_ends(values, own_key, least, top_value):
    index_at = [jax.random.randint(jax.random.fold_in(own_key, axis), (), 0, length) for axis, length in enumerate(values.shape)]
    widest = values.shape.index(max(values.shape))
    next_to = index_at[:widest] + [(index_at[widest] + 1) % values.shape[widest]] + index_at[widest + 1:]
    return values.at[tuple(index_at)].set(least).at[tuple(next_to)].set(top_value)


def level_of(stream_key, shape, shards, low, largest):
    def one(position, blocks):
        draws = jax.random.uniform(jax.random.fold_in(jax.random.fold_in(stream_key, 6), position), (blocks,), jnp.float32, low / len(shards), largest / len(shards))
        return jnp.repeat(jnp.exp(draws), shape[position] // blocks).reshape((-1,) + (1,) * (len(shape) - position - 1))

    gain = one(*shards[0])
    for cut in shards[1:]:
        gain = gain * one(*cut)
    return gain


def normal_values(key, dims, width, most, pieces=(), held_as=jnp.bfloat16):
    factor_of = level_of(key, dims, pieces, -0.22, 0.18) if pieces else 1.0
    drawn = jax.random.normal(key, dims, jnp.float32) * width * factor_of
    return jnp.minimum(jnp.maximum(drawn, -most), most).astype(held_as)


def setup_inputs(seed: int = 0) -> dict:
    key_list = jax.random.split(jax.random.key(seed), 7)
    return {
        "atmos_state": draw_atmos_state(jax.random.fold_in(key_list[6], 71), 0),
        "horiz_wind": normal_values(key_list[1], (2, LEV, NX, NY), 1.0, 6.0, ((2, 4), (3, 32)), jnp.float32),
        "route_map": draw_route_map(jax.random.fold_in(key_list[6], 71), 0),
        "diffusivity": draw_diffusivity(jax.random.fold_in(key_list[6], 71), 0),
        "branch_mask": touch_ends(jax.random.randint(key_list[4], (LEV, SLOTS), 0, 4), jax.random.fold_in(key_list[4], 1), 0, 3).astype(jnp.int32),
        "phys_state": normal_values(key_list[5], (PF, LEV, SLOTS), 1.0, 6.0, ((2, 128),), jnp.float32),
    }


PENALTY = 3.0
STEP_SIZE = 0.05
LATENT_WARM = 0.5
LATENT_ICE = 0.6
COUPLE_WARM = [0.8, -0.6, 0.5, 0.9, -0.7, 0.4, 1.0, -0.5]
COUPLE_ICE = [-0.4, 0.7, 0.9, -0.5, 0.6, -0.8, 0.3, 0.7]

def gll_matrix():
    node_points = np.array([-1.0, -1.0 / np.sqrt(5.0), 1.0 / np.sqrt(5.0), 1.0])
    products = np.ones(4)
    for row_at in range(4):
        for other_at in range(4):
            if other_at != row_at:
                products[row_at] = products[row_at] * (node_points[row_at] - node_points[other_at])
    result_table = np.zeros((4, 4))
    for row_at in range(4):
        for col_at in range(4):
            if row_at != col_at:
                result_table[row_at, col_at] = products[row_at] / (products[col_at] * (node_points[row_at] - node_points[col_at]))
            else:
                diagonal_sum = 0.0
                for other_at in range(4):
                    if other_at != row_at:
                        diagonal_sum = diagonal_sum + 1.0 / (node_points[row_at] - node_points[other_at])
                result_table[row_at, col_at] = diagonal_sum
    return result_table

def element_grad(padded, axis_at):
    extent = padded.shape[axis_at] - 2
    interior = lax.slice_in_dim(padded, 1, extent + 1, axis=axis_at)
    below_edge = lax.slice_in_dim(padded, 0, extent, NP, axis=axis_at)
    above_edge = lax.slice_in_dim(padded, NP + 1, extent + 2, NP, axis=axis_at)
    interior = jnp.moveaxis(interior, axis_at, -1)
    below_edge = jnp.moveaxis(below_edge, axis_at, -1)
    above_edge = jnp.moveaxis(above_edge, axis_at, -1)
    dims_full = interior.shape
    element_blocks = interior.reshape(dims_full[:-1] + (extent // NP, NP))
    deriv_table = jnp.asarray(gll_matrix(), jnp.float32)
    gradient = jnp.einsum('...ej,ij->...ei', element_blocks, deriv_table, precision=lax.Precision.HIGHEST)
    gradient = gradient.at[..., 0].add(-PENALTY * (below_edge - element_blocks[..., 0]))
    gradient = gradient.at[..., NP - 1].add(PENALTY * (above_edge - element_blocks[..., NP - 1]))
    return jnp.moveaxis(gradient.reshape(dims_full), -1, axis_at)

def thomas_solve(rhs_in, coupling):
    zero_row = jnp.zeros_like(coupling[:1])
    sub_diag = jnp.concatenate([zero_row, -coupling[:-1]], 0)
    super_diag = jnp.concatenate([-coupling[:-1], zero_row], 0)
    main_diag = 1.0 + coupling + jnp.concatenate([zero_row, coupling[:-1]], 0)

    def forward(carry, level_in):
        prev_upper, prev_value = carry
        sub_at, main_at, super_at, rhs_at = level_in
        pivot = main_at - sub_at * prev_upper
        next_upper = super_at / pivot
        next_value = (rhs_at - sub_at * prev_value) / pivot
        return ((next_upper, next_value), (next_upper, next_value))
    start_carry = (jnp.zeros_like(coupling[0]), jnp.zeros_like(rhs_in[:, 0]))
    unused, (upper_star, value_star) = lax.scan(forward, start_carry, (sub_diag, main_diag, super_diag, jnp.moveaxis(rhs_in, 1, 0)))

    def backward(carry, level_in):
        upper_at, value_at = level_in
        result_value = value_at - upper_at * carry
        return (result_value, result_value)
    unused, solved = lax.scan(backward, jnp.zeros_like(rhs_in[:, 0]), (upper_star, value_star), reverse=True)
    return jnp.moveaxis(solved, 0, 1)

def microphysics(solved, rate_warm, rate_ice):
    current = solved
    warm_total = jnp.zeros_like(rate_warm)
    ice_total = jnp.zeros_like(rate_ice)
    for pass_num in range(NPASS):
        denominator = 1.0 + rate_warm + rate_ice
        vapour = current[1]
        to_warm = rate_warm * vapour / denominator
        to_ice = rate_ice * vapour / denominator
        current = jnp.concatenate([(current[0] + LATENT_WARM * to_warm + LATENT_ICE * to_ice)[None], (vapour - to_warm - to_ice)[None], (current[2] + to_warm)[None], (current[3] + to_ice)[None], current[4:]], 0)
        warm_total = warm_total + to_warm
        ice_total = ice_total + to_ice
    return (current, warm_total, ice_total)

def column_physics(inputs):
    column_state, coupling, rate_warm, rate_ice = inputs
    solved = thomas_solve(column_state, coupling)
    after, warm_total, ice_total = microphysics(solved, rate_warm, rate_ice)
    return ((after - column_state).astype(jnp.bfloat16), warm_total, ice_total)

def to_devices(grid):
    leading = grid.shape[:-2]
    count_lead = len(leading)
    split = grid.reshape(leading + (N_EDGE, X_DEV, N_COLS, Y_DEV))
    split = jnp.moveaxis(split, count_lead + 2, count_lead + 1)
    return split.reshape(leading + (N_EDGE * N_COLS, X_DEV * Y_DEV))

def from_devices(stacked):
    leading = stacked.shape[:-2]
    count_lead = len(leading)
    split = stacked.reshape(leading + (N_EDGE, N_COLS, X_DEV, Y_DEV))
    split = jnp.moveaxis(split, count_lead + 1, count_lead + 2)
    return split.reshape(leading + (X_DEV * N_EDGE, Y_DEV * N_COLS))

def reference(atmos_state, horiz_wind, route_map, diffusivity, branch_mask, phys_state):
    state_f = atmos_state.astype(jnp.float32)
    padded_x = jnp.concatenate([state_f[:, :, -1:], state_f, state_f[:, :, :1]], 2)
    padded_y = jnp.concatenate([state_f[:, :, :, -1:], state_f, state_f[:, :, :, :1]], 3)
    grad_x = element_grad(padded_x, 2)
    grad_y = element_grad(padded_y, 3)
    tendency = -(horiz_wind[0] * grad_x + horiz_wind[1] * grad_y)
    destination = to_devices(route_map)
    device_count = N_EDGE * N_COLS
    onehot = (destination[:, :, None] == jnp.arange(N_COLS, dtype=jnp.int32)[None, None, :]).astype(jnp.int32)
    rank_in = lax.optimization_barrier(jnp.sum((jnp.cumsum(onehot, 1) - onehot) * onehot, 2))
    device_ids = jnp.arange(device_count, dtype=jnp.int32)[:, None]
    edge_ids = device_ids // N_COLS
    source_ids = device_ids % N_COLS
    slot_of = (((edge_ids * N_COLS + destination) * N_COLS + source_ids) * CAP + rank_in).astype(jnp.int32)
    flat_slot = slot_of.reshape(-1)
    columns = X_DEV * Y_DEV

    def at_slots(table):
        picked = table[:, flat_slot].reshape(LEV, device_count, columns)
        return jnp.moveaxis(picked, 1, 0)
    coupling = at_slots(diffusivity)
    rate_warm = at_slots(jax.nn.softplus(phys_state[0]) * (branch_mask % 2).astype(jnp.float32))
    rate_ice = at_slots(jax.nn.softplus(phys_state[1]) * (branch_mask // 2).astype(jnp.float32))
    column_state = jnp.moveaxis(to_devices(state_f), 2, 0)
    increment, warm_total, ice_total = lax.map(column_physics, (column_state, coupling, rate_warm, rate_ice))
    increment_grid = from_devices(jnp.moveaxis(increment, 0, 2))
    new_state = (state_f + STEP_SIZE * tendency + increment_grid.astype(jnp.float32)).astype(jnp.bfloat16)
    warm_slots = jnp.zeros((LEV, SLOTS), jnp.float32).at[:, flat_slot].set(jnp.moveaxis(warm_total, 0, 1).reshape(LEV, -1))
    ice_slots = jnp.zeros((LEV, SLOTS), jnp.float32).at[:, flat_slot].set(jnp.moveaxis(ice_total, 0, 1).reshape(LEV, -1))
    couple_warm = jnp.asarray(COUPLE_WARM, jnp.float32)[:, None, None]
    couple_ice = jnp.asarray(COUPLE_ICE, jnp.float32)[:, None, None]
    phys_next = phys_state + couple_warm * warm_slots[None] + couple_ice * ice_slots[None]
    return (new_state, phys_next)
```

```python
import functools

import jax
import jax.numpy as jnp
import numpy as np
from jax import lax
from jax.experimental import pallas as pl
from jax.experimental.pallas import tpu as pltpu
from jax.sharding import PartitionSpec as P

MESH = pl.DeviceIdType.MESH
F32, BF16 = jnp.float32, jnp.bfloat16
FIELDS, LEV, XD, YD = 11, 128, 4, 128
EDGE, COLS, CAP, PF = 4, 32, 32, 8
SLOTS = COLS * CAP
ROWS = LEV * XD
ALL_ROWS = FIELDS * ROWS
CHUNK = 128
CHUNKS = ALL_ROWS // CHUNK
CLEV = CHUNK // XD
YPAD = 48
PENALTY = 3.0
STEP_SIZE = 0.05
LATENT_WARM = 0.5
LATENT_ICE = 0.6
COUPLE_WARM = [0.8, -0.6, 0.5, 0.9, -0.7, 0.4, 1.0, -0.5]
COUPLE_ICE = [-0.4, 0.7, 0.9, -0.5, 0.6, -0.8, 0.3, 0.7]


def gll_matrix():
    nodes = np.array([-1.0, -1.0 / np.sqrt(5.0), 1.0 / np.sqrt(5.0), 1.0])
    prod = [np.prod([nodes[i] - nodes[j] for j in range(4) if j != i]) for i in range(4)]
    table = np.zeros((4, 4))
    for i in range(4):
        for j in range(4):
            if i != j:
                table[i, j] = prod[i] / (prod[j] * (nodes[i] - nodes[j]))
            else:
                table[i, i] = sum(1.0 / (nodes[i] - nodes[k]) for k in range(4) if k != i)
    return table


def split_bf16(table):
    high = table.astype(np.float32).astype(BF16)
    low = (table - high.astype(np.float64)).astype(np.float32).astype(BF16)
    return high, low


def constants():
    own = gll_matrix()
    own[0, 0] += PENALTY
    own[3, 3] -= PENALTY
    gx = np.zeros((CHUNK, CHUNK + 2 * CLEV))
    for lev in range(CLEV):
        gx[4 * lev : 4 * lev + 4, 4 * lev : 4 * lev + 4] = own
        gx[4 * lev, CHUNK + lev] = -PENALTY
        gx[4 * lev + 3, CHUNK + CLEV + lev] = PENALTY
    gy = np.zeros((YD, YD))
    for el in range(YD // 4):
        gy[4 * el : 4 * el + 4, 4 * el : 4 * el + 4] = own.T
        if el:
            gy[4 * el - 1, 4 * el] = -PENALTY
        if el < YD // 4 - 1:
            gy[4 * el + 4, 4 * el + 3] = PENALTY
    ey = np.zeros((YD, YD))
    ey[:YPAD, 0] = -PENALTY
    ey[YPAD : 2 * YPAD, YD - 1] = PENALTY
    pick = np.zeros((16, YD))
    pick[0, 0] = 1
    pick[8, YD - 1] = 1
    tri = np.triu(np.ones((YD, YD)), 1)
    eye = np.eye(128)
    gx = (-STEP_SIZE) * gx
    gy = (-STEP_SIZE) * gy
    ey = (-STEP_SIZE) * ey
    out = [*split_bf16(gx), *split_bf16(gy), *split_bf16(ey)]
    return out + [pick.astype(BF16), tri.astype(BF16), eye.astype(BF16)]


def far_first():
    def dist(k):
        z, y = k // 8, (k // 2) % 4
        return min(z, 4 - z) + min(y, 4 - y)

    return sorted(range(1, COLS), key=lambda k: -dist(k))


def softplus(x):
    return jnp.maximum(x, 0.0) + jnp.log1p(jnp.exp(-jnp.abs(x)))


def rates(phys0, phys1, mask):
    warm = jnp.where((mask & 1) == 1, softplus(phys0), 0.0)
    ice = jnp.where(mask >= 2, softplus(phys1), 0.0)
    return warm, ice


def dot(a, b):
    return jnp.dot(a, b, preferred_element_type=F32)


def dot_t(a, b):
    return lax.dot_general(a, b, (((1,), (1,)), ((), ())), preferred_element_type=F32)


def t_dot(a, b):
    return lax.dot_general(a, b, (((0,), (0,)), ((), ())), preferred_element_type=F32)


def exchange_kernel(
    q, route, kv, mask, phys, wind, gxh, gxl, gyh, gyl, eyh, eyl, pick, tri, eye,
    recv, tend, slots,
    snd, qf, xs, xr, ysf, ys, yr, ss, rs, hss, hrs,
):
    e, me = lax.axis_index("edge"), lax.axis_index("cols")
    core, yy, zz = me % 2, (me // 2) % 4, me // 8
    order = far_first()

    def peer(k):
        return ((zz + k // 8) % 4) * 8 + ((yy + (k // 2) % 4) % 4) * 2 + (core + k % 2) % 2

    up_x, down_x = (e + 1) % EDGE, (e + EDGE - 1) % EDGE
    up_y, down_y = (me + 1) % COLS, (me + COLS - 1) % COLS
    bar = pltpu.get_barrier_semaphore()
    for k in order:
        pl.semaphore_signal(bar, inc=1, device_id=(e, peer(k)), device_id_type=MESH)
    for to in (up_x, down_x):
        pl.semaphore_signal(bar, inc=1, device_id=(to, me), device_id_type=MESH)

    def tile(j, carry):
        lanes = pl.ds(pl.multiple_of(j * 128, 128), 128)
        warm, ice = rates(phys[0, :, lanes], phys[1, :, lanes], mask[:, lanes])
        for v, value in ((0, kv[:, lanes]), (2, warm), (3, ice)):
            turned = dot_t(eye[...], value.astype(BF16)).astype(BF16)
            snd[pl.ds(j * 4, 4), v] = turned.reshape(4, CAP, LEV)
        return carry

    lax.fori_loop(0, 8, tile, 0)

    dest_at = lax.broadcasted_iota(jnp.int32, (COLS, YD), 0)
    before = jnp.zeros((COLS, 1), F32)
    for x in range(XD):
        hot = dest_at == route[x : x + 1, :]
        hot_f = jnp.where(hot, 1.0, 0.0)
        earlier = dot(hot_f.astype(BF16), tri[...]) + before
        before = before + jnp.sum(hot_f, axis=1, keepdims=True)
        rank = jnp.sum(jnp.where(hot, earlier, 0.0), axis=0, keepdims=True)
        slots[x : x + 1, :] = route[x : x + 1, :] * CAP + rank.astype(jnp.int32)

    qf[...] = q[...].astype(F32)
    for i, x in enumerate((0, XD - 1)):
        xs[i] = qf[pl.ds(x, FIELDS * LEV, stride=XD), :].astype(BF16)
    slot_at = lax.broadcasted_iota(jnp.int32, (SLOTS, YD), 0)
    total = jnp.zeros((SLOTS, LEV), F32)
    for x in range(XD):
        hot = jnp.where(slot_at == slots[x : x + 1, :], 1.0, 0.0).astype(BF16)
        vapour = qf[pl.ds(ROWS + x, LEV, stride=XD), :].astype(BF16)
        total = total + dot_t(hot, vapour)
    snd[:, 1] = total.astype(BF16).reshape(COLS, CAP, LEV)

    def edge_points(c, carry):
        rows = pl.ds(pl.multiple_of(c * CHUNK, CHUNK), CHUNK)
        ends = dot_t(pick[...], q[rows, :])
        ysf[pl.ds(c, 1), :] = ends[0:1]
        ysf[pl.ds(YPAD + c, 1), :] = ends[8:9]
        return carry

    ysf[...] = jnp.zeros_like(ysf)
    lax.fori_loop(0, CHUNKS, edge_points, 0)
    ys[...] = ysf[...].astype(BF16)

    pl.semaphore_wait(bar, COLS - 1 + 2)
    copies = []
    for i, to in ((0, down_x), (1, up_x)):
        copies.append(
            pltpu.make_async_remote_copy(
                xs.at[i], xr.at[1 - i], hss.at[i], hrs.at[1 - i],
                device_id=(to, me), device_id_type=MESH,
            )
        )
    for i, to in ((0, down_y), (1, up_y)):
        copies.append(
            pltpu.make_async_remote_copy(
                ys.at[pl.ds(i * YPAD, YPAD)], yr.at[pl.ds((1 - i) * YPAD, YPAD)],
                hss.at[2 + i], hrs.at[3 - i],
                device_id=(e, to), device_id_type=MESH,
            )
        )
    for c in copies:
        c.start()

    def message(k):
        to = peer(k)
        return pltpu.make_async_remote_copy(
            snd.at[to], recv.at[me], ss.at[k], rs.at[k],
            device_id=(e, to), device_id_type=MESH,
        )

    for k in order:
        message(k).start()
    recv[pl.ds(me, 1)] = snd[pl.ds(me, 1)]
    yr[2 * YPAD :, :] = jnp.zeros((YD - 2 * YPAD, YD), BF16)
    for c in copies:
        c.wait()

    y_halo = dot_t(eye[...], yr[...])
    lane = lax.broadcasted_iota(jnp.int32, (CHUNK, YD), 1)

    def dynamics(c, carry):
        rows = pl.ds(pl.multiple_of(c * CHUNK, CHUNK), CHUNK)
        levels = pl.ds(pl.multiple_of(c * CLEV, CLEV), CLEV)
        wrows = pl.ds(pl.multiple_of((c % (ROWS // CHUNK)) * CHUNK, CHUNK), CHUNK)
        mine = q[rows, :]
        around = jnp.concatenate([mine, xr[0, levels], xr[1, levels]], axis=0)
        dx = dot(gxh[...], around) + dot(gxl[...], around)
        ends = jnp.where((lane == c) | (lane == YPAD + c), y_halo, 0.0).astype(BF16)
        dy = dot(mine, gyh[...]) + dot(mine, gyl[...])
        dy = dy + dot(ends, eyh[...]) + dot(ends, eyl[...])
        tend[rows, :] = (wind[0, wrows] * dx + wind[1, wrows] * dy).astype(BF16)
        return carry

    lax.fori_loop(0, CHUNKS, dynamics, 0)
    for k in order:
        message(k).wait()


def column_kernel(
    recv, slots, q, tend, kv, mask, phys, eye, new, phys_out, sol, cu, par, group, gkv, gcu
):
    slot_at = lax.broadcasted_iota(jnp.int32, (SLOTS, YD), 0)
    for x in range(XD):
        hot = jnp.where(slot_at == slots[x : x + 1, :], 1.0, 0.0).astype(BF16)
        for i, v in enumerate((0, 2, 3)):
            par[i, pl.ds(x * LEV, LEV), :] = t_dot(recv[:, v].reshape(SLOTS, LEV), hot)
    sol[...] = q[...].astype(F32)
    for j in range(8):
        rows = pl.ds(j * LEV, LEV)
        vapour = recv[pl.ds(j * 4, 4), 1].reshape(128, LEV)
        group[rows, :] = dot_t(eye[...], vapour)
        gkv[rows, :] = kv[:, j * 128 : (j + 1) * 128]

    def forward(k, carry):
        kv_t, cu_t, kv_g, cu_g, prev, prev_g = carry
        here = par[0, pl.ds(k, XD, stride=LEV), :]
        inv = 1.0 / (1.0 + here + kv_t - kv_t * cu_t)
        low = kv_t * inv
        cu_t = here * inv
        at = pl.multiple_of(k * XD, XD)
        cu[pl.ds(at, XD), :] = cu_t
        values = []
        for f in range(FIELDS):
            rows = pl.ds(f * ROWS + at, XD)
            value = sol[rows, :] * inv + low * prev[f]
            sol[rows, :] = value
            values.append(value)
        here_g = gkv[pl.ds(k, 8, stride=LEV), :]
        inv_g = 1.0 / (1.0 + here_g + kv_g - kv_g * cu_g)
        low_g = kv_g * inv_g
        cu_g = here_g * inv_g
        gcu[pl.ds(pl.multiple_of(k * 8, 8), 8), :] = cu_g
        value_g = group[pl.ds(k, 8, stride=LEV), :] * inv_g + low_g * prev_g
        group[pl.ds(k, 8, stride=LEV), :] = value_g
        return here, cu_t, here_g, cu_g, tuple(values), value_g

    zt, zg = jnp.zeros((XD, YD), F32), jnp.zeros((8, 128), F32)
    lax.fori_loop(0, LEV, forward, (zt, zt, zg, zg, (zt,) * FIELDS, zg), unroll=4)

    def backward(i, carry):
        after, after_g = carry
        k = LEV - 1 - i
        at = pl.multiple_of(k * XD, XD)
        cu_t = cu[pl.ds(at, XD), :]
        values = []
        for f in range(FIELDS):
            rows = pl.ds(f * ROWS + at, XD)
            value = sol[rows, :] + cu_t * after[f]
            sol[rows, :] = value
            values.append(value)
        cu_g = gcu[pl.ds(pl.multiple_of(k * 8, 8), 8), :]
        value_g = group[pl.ds(k, 8, stride=LEV), :] + cu_g * after_g
        group[pl.ds(k, 8, stride=LEV), :] = value_g
        return tuple(values), value_g

    lax.fori_loop(0, LEV, backward, ((zt,) * FIELDS, zg), unroll=4)

    for x in range(XD):
        warm, ice = par[1, pl.ds(x * LEV, LEV), :], par[2, pl.ds(x * LEV, LEV), :]
        inv = 1.0 / (1.0 + warm + ice)
        rows = [pl.ds(f * ROWS + x, LEV, stride=XD) for f in range(4)]
        passes = sol[rows[1], :] * (inv + inv * inv)
        to_warm, to_ice = warm * passes, ice * passes
        sol[rows[0], :] += LATENT_WARM * to_warm + LATENT_ICE * to_ice
        sol[rows[1], :] -= to_warm + to_ice
        sol[rows[2], :] += to_warm
        sol[rows[3], :] += to_ice
    new[...] = (sol[...] + tend[...].astype(F32)).astype(BF16)

    for j in range(8):
        lanes = slice(j * 128, (j + 1) * 128)
        warm, ice = rates(phys[0, :, lanes], phys[1, :, lanes], mask[:, lanes])
        inv = 1.0 / (1.0 + warm + ice)
        passes = group[j * LEV : (j + 1) * LEV, :] * (inv + inv * inv)
        warm, ice = warm * passes, ice * passes
        for f in range(PF):
            phys_out[f, :, lanes] = (
                phys[f, :, lanes] + COUPLE_WARM[f] * warm + COUPLE_ICE[f] * ice
            )


def shards(atmos_state, horiz_wind, route_map, diffusivity, branch_mask, phys_state):
    q = atmos_state.reshape(ALL_ROWS, YD)
    wind = horiz_wind.reshape(2, ROWS, YD)
    consts = [jnp.asarray(c) for c in constants()]
    whole = pl.BlockSpec(memory_space=pltpu.VMEM)
    recv, tend, slots = pl.pallas_call(
        exchange_kernel,
        grid=(1,),
        out_shape=(
            jax.ShapeDtypeStruct((COLS, 4, CAP, LEV), BF16),
            jax.ShapeDtypeStruct((ALL_ROWS, YD), BF16),
            jax.ShapeDtypeStruct((XD, YD), jnp.int32),
        ),
        in_specs=[whole] * 4
        + [pl.BlockSpec((2, LEV, SLOTS), lambda i: (0, 0, 0))]
        + [whole] * (1 + len(consts)),
        out_specs=(whole,) * 3,
        scratch_shapes=[
            pltpu.VMEM((COLS, 4, CAP, LEV), BF16),
            pltpu.VMEM((ALL_ROWS, YD), F32),
            pltpu.VMEM((2, FIELDS * LEV, YD), BF16),
            pltpu.VMEM((2, FIELDS * LEV, YD), BF16),
            pltpu.VMEM((2 * YPAD, YD), F32),
            pltpu.VMEM((2 * YPAD, YD), BF16),
            pltpu.VMEM((YD, YD), BF16),
            pltpu.SemaphoreType.DMA((COLS,)),
            pltpu.SemaphoreType.DMA((COLS,)),
            pltpu.SemaphoreType.DMA((4,)),
            pltpu.SemaphoreType.DMA((4,)),
        ],
        compiler_params=pltpu.CompilerParams(
            collective_id=0, has_side_effects=True, vmem_limit_bytes=40 << 20
        ),
    )(q, route_map, diffusivity, branch_mask, phys_state, wind, *consts)
    new, phys_next = pl.pallas_call(
        column_kernel,
        out_shape=(
            jax.ShapeDtypeStruct((ALL_ROWS, YD), BF16),
            jax.ShapeDtypeStruct((PF, LEV, SLOTS), F32),
        ),
        in_specs=[whole] * 8,
        out_specs=(whole,) * 2,
        scratch_shapes=[
            pltpu.VMEM((ALL_ROWS, YD), F32),
            pltpu.VMEM((ROWS, YD), F32),
            pltpu.VMEM((3, XD * LEV, YD), F32),
            pltpu.VMEM((8 * LEV, 128), F32),
            pltpu.VMEM((8 * LEV, 128), F32),
            pltpu.VMEM((8 * LEV, 128), F32),
        ],
        compiler_params=pltpu.CompilerParams(vmem_limit_bytes=40 << 20),
    )(recv, slots, q, tend, diffusivity, branch_mask, phys_state, consts[-1])
    return new.reshape(FIELDS, LEV, XD, YD), phys_next


def solution(mesh):
    return jax.shard_map(
        shards,
        mesh=mesh,
        in_specs=(
            P(None, None, "edge", "cols"),
            P(None, None, "edge", "cols"),
            P("edge", "cols"),
            P(None, ("edge", "cols")),
            P(None, ("edge", "cols")),
            P(None, None, ("edge", "cols")),
        ),
        out_specs=(P(None, None, "edge", "cols"), P(None, None, ("edge", "cols"))),
        check_vma=False,
    )
```

```python
import functools

import jax
import jax.numpy as jnp
import numpy as np
from jax import lax
from jax.experimental import pallas as pl
from jax.experimental.pallas import tpu as pltpu
from jax.sharding import PartitionSpec as P

MESH = pl.DeviceIdType.MESH
F32, BF16 = jnp.float32, jnp.bfloat16
FIELDS, LEV, XD, YD = 11, 128, 4, 128
EDGE, COLS, CAP, PF = 4, 32, 32, 8
SLOTS = COLS * CAP
ROWS = LEV * XD
ALL_ROWS = FIELDS * ROWS
TOP = 4
YPAD = 16
PENALTY = 3.0
STEP_SIZE = 0.05
LATENT_WARM = 0.5
LATENT_ICE = 0.6
COUPLE_WARM = [0.8, -0.6, 0.5, 0.9, -0.7, 0.4, 1.0, -0.5]
COUPLE_ICE = [-0.4, 0.7, 0.9, -0.5, 0.6, -0.8, 0.3, 0.7]


def gll_matrix():
    nodes = np.array([-1.0, -1.0 / np.sqrt(5.0), 1.0 / np.sqrt(5.0), 1.0])
    prod = [np.prod([nodes[i] - nodes[j] for j in range(4) if j != i]) for i in range(4)]
    table = np.zeros((4, 4))
    for i in range(4):
        for j in range(4):
            if i != j:
                table[i, j] = prod[i] / (prod[j] * (nodes[i] - nodes[j]))
            else:
                table[i, i] = sum(1.0 / (nodes[i] - nodes[k]) for k in range(4) if k != i)
    return table


def split_bf16(table):
    high = table.astype(np.float32).astype(BF16)
    low = (table - high.astype(np.float64)).astype(np.float32).astype(BF16)
    return high, low


def derivative():
    own = gll_matrix()
    own[0, 0] += PENALTY
    own[3, 3] -= PENALTY
    return -STEP_SIZE * own


def constants():
    own = derivative() / -STEP_SIZE
    gy = np.zeros((YD, YD))
    for el in range(YD // 4):
        gy[4 * el : 4 * el + 4, 4 * el : 4 * el + 4] = own.T
        if el:
            gy[4 * el - 1, 4 * el] = -PENALTY
        if el < YD // 4 - 1:
            gy[4 * el + 4, 4 * el + 3] = PENALTY
    ey = np.zeros((YD, YD))
    ey[:YPAD, 0] = -PENALTY
    ey[YPAD : 2 * YPAD, YD - 1] = PENALTY
    table = np.concatenate(split_bf16(-STEP_SIZE * np.concatenate([gy, ey], 0)), 1)
    tri = np.triu(np.ones((YD, YD)), 1)
    square = np.concatenate([tri, np.eye(128)], 1).astype(BF16)
    return np.concatenate([table, square], 0)


def far_first():
    def dist(k):
        z, y = k // 8, (k // 2) % 4
        return min(z, 4 - z) + min(y, 4 - y)

    return sorted(range(1, COLS), key=lambda k: -dist(k))


def softplus(x):
    return jnp.maximum(x, 0.0) + jnp.log1p(jnp.exp(-jnp.abs(x)))


def rates(phys0, phys1, mask):
    warm = jnp.where((mask & 1) == 1, softplus(phys0), 0.0)
    ice = jnp.where(mask >= 2, softplus(phys1), 0.0)
    return warm, ice


def dot(a, b):
    return jnp.dot(a, b, preferred_element_type=F32)


def dot_t(a, b):
    return lax.dot_general(a, b, (((1,), (1,)), ((), ())), preferred_element_type=F32)


def t_dot(a, b):
    return lax.dot_general(a, b, (((0,), (0,)), ((), ())), preferred_element_type=F32)


def exchange_kernel(
    q_h, route_h, kv_h, mask_h, phys_h, wind_h, const_h,
    recv_b, hot, pre, vap, rest, phys,
    qv, route, kv, mask, wind, const, group, in_sem,
    snd_a, snd_b, recv_a, sol, qp, tn, xr, ys, yr, wp, par, cu, gkv, gcu,
    ss, rs, hss, hrs,
):
    e, me = lax.axis_index("edge"), lax.axis_index("cols")
    core, yy, zz = me % 2, (me // 2) % 4, me // 8
    order = far_first()

    def peer(k):
        return ((zz + k // 8) % 4) * 8 + ((yy + (k // 2) % 4) % 4) * 2 + (core + k % 2) % 2

    up_x, down_x = (e + 1) % EDGE, (e + EDGE - 1) % EDGE
    up_y, down_y = (me + 1) % COLS, (me + COLS - 1) % COLS
    loads = [
        pltpu.make_async_copy(a, b, in_sem.at[i])
        for i, (a, b) in enumerate(
            (
                (const_h, const), (kv_h, kv), (route_h, route), (q_h, qv),
                (mask_h, mask), (phys_h, phys), (wind_h, wind),
            )
        )
    ]
    for c in loads:
        c.start()
    bar = pltpu.get_barrier_semaphore()
    for k in order:
        pl.semaphore_signal(bar, inc=1, device_id=(e, peer(k)), device_id_type=MESH)
    for to in (up_x, down_x):
        pl.semaphore_signal(bar, inc=1, device_id=(to, me), device_id_type=MESH)
    tri = const.at[pl.ds(256, 128), pl.ds(0, 128)]
    eye = const.at[pl.ds(256, 128), pl.ds(128, 128)]

    def turn(j, value):
        turned = dot_t(eye[...], value.astype(BF16)).astype(BF16)
        return turned.reshape(4, CAP, LEV)

    loads[0].wait()
    loads[1].wait()
    for j in range(8):
        snd_a[4 * j : 4 * j + 4, 0] = turn(j, kv[:, j * 128 : (j + 1) * 128])

    loads[2].wait()
    dest_at = lax.broadcasted_iota(jnp.int32, (COLS, YD), 0)
    slot_at = lax.broadcasted_iota(jnp.int32, (SLOTS, YD), 0)
    before = jnp.zeros((COLS, 1), F32)
    for x in range(XD):
        chosen = dest_at == route[x : x + 1, :]
        chosen_f = jnp.where(chosen, 1.0, 0.0)
        earlier = dot(chosen_f.astype(BF16), tri[...]) + before
        before = before + jnp.sum(chosen_f, axis=1, keepdims=True)
        rank = jnp.sum(jnp.where(chosen, earlier, 0.0), axis=0, keepdims=True)
        slots = route[x : x + 1, :] * CAP + rank.astype(jnp.int32)
        hot[:, x * YD : (x + 1) * YD] = jnp.where(slot_at == slots, 1.0, 0.0).astype(BF16)

    loads[3].wait()

    def planes(f, carry):
        rows = pl.ds(pl.multiple_of(f * ROWS, ROWS), ROWS)
        sol[rows, :] = qv[rows, :].astype(F32)
        for x in range(XD):
            qp[f, x] = sol[pl.ds(f * ROWS + x, LEV, stride=XD), :].astype(BF16)
        return carry

    lax.fori_loop(0, FIELDS, planes, 0)
    total = dot_t(hot[...], jnp.concatenate([qp[1, x] for x in range(XD)], axis=1))
    snd_a[:, 1] = total.astype(BF16).reshape(COLS, CAP, LEV)

    fields = jnp.concatenate([qp[f].reshape(ROWS, YD) for f in range(FIELDS)], axis=1)
    at = lax.broadcasted_iota(jnp.int32, (YD, YD), 0)
    lane = lax.broadcasted_iota(jnp.int32, (YD, YD), 1)
    pick = [
        jnp.where(((at == 0) & (lane == f)) | ((at == YD - 1) & (lane == YPAD + f)), 1.0, 0.0)
        for f in range(FIELDS)
    ]
    ends = dot(fields, jnp.concatenate(pick, axis=0).astype(BF16)).astype(BF16)
    ys[...] = dot_t(eye[0 : 2 * YPAD, :], ends).astype(BF16)

    pl.semaphore_wait(bar, COLS - 1 + 2)
    y_copies, x_copies = [], []
    for i, to in ((0, down_y), (1, up_y)):
        y_copies.append(
            pltpu.make_async_remote_copy(
                ys.at[pl.ds(i * YPAD, YPAD)], yr.at[pl.ds((1 - i) * YPAD, YPAD)],
                hss.at[2 + i], hrs.at[3 - i],
                device_id=(e, to), device_id_type=MESH,
            )
        )
    for i, to in ((0, down_x), (1, up_x)):
        x_copies.append(
            pltpu.make_async_remote_copy(
                qp.at[:, i * (XD - 1)], xr.at[1 - i], hss.at[i], hrs.at[1 - i],
                device_id=(to, me), device_id_type=MESH,
            )
        )
    for c in y_copies + x_copies:
        c.start()

    def message(k, part):
        to = peer(k)
        source, target = ((snd_a, recv_a), (snd_b, recv_b))[part]
        return pltpu.make_async_remote_copy(
            source.at[to], target.at[me], ss.at[part, k], rs.at[part, k],
            device_id=(e, to), device_id_type=MESH,
        )

    for k in order:
        message(k, 0).start()
    loads[4].wait()
    loads[5].wait()
    for j in range(8):
        lanes = slice(j * 128, (j + 1) * 128)
        warm, ice = rates(phys[0, :, lanes], phys[1, :, lanes], mask[:, lanes])
        snd_b[4 * j : 4 * j + 4, 0] = turn(j, warm)
        snd_b[4 * j : 4 * j + 4, 1] = turn(j, ice)
    for k in order:
        message(k, 1).start()
    recv_a[pl.ds(me, 1)] = snd_a[pl.ds(me, 1)]
    recv_b[pl.ds(me, 1)] = snd_b[pl.ds(me, 1)]

    loads[6].wait()
    for i in range(2):
        for x in range(XD):
            wp[i, x] = wind[i, pl.ds(x, LEV, stride=XD), :]
    for c in y_copies:
        c.wait()
    y_halo = t_dot(yr[...], eye[0 : 2 * YPAD, :])
    wide = lax.broadcasted_iota(jnp.int32, (ROWS, YD), 1)
    along = derivative()

    def dynamics(f, carry):
        near = jnp.where((wide == f) | (wide == YPAD + f), y_halo, 0.0).astype(BF16)
        both = jnp.concatenate([qp[f].reshape(ROWS, YD), near], axis=1)
        dy = dot(both, const[0:256, :])
        own = [qp[f, x].astype(F32) for x in range(XD)]
        for x in range(XD):
            dx = sum(float(along[x, i]) * own[i] for i in range(XD) if abs(along[x, i]) > 1e-9)
            rows = slice(x * LEV, (x + 1) * LEV)
            tn[pl.ds(f * ROWS + x, LEV, stride=XD), :] = wp[0, x] * dx + wp[1, x] * (
                dy[rows, :YD] + dy[rows, YD:]
            )
        return carry

    lax.fori_loop(0, FIELDS, dynamics, 0)

    for k in order:
        message(k, 0).wait()
    here = t_dot(recv_a[:, 0].reshape(SLOTS, LEV), hot[...])
    for x in range(XD):
        par[x * LEV : (x + 1) * LEV, :] = here[:, x * YD : (x + 1) * YD]
    for j in range(8):
        rows = pl.ds(j * LEV, LEV)
        group[rows, :] = dot_t(eye[...], recv_a[4 * j : 4 * j + 4, 1].reshape(128, LEV))
        gkv[rows, :] = kv[:, j * 128 : (j + 1) * 128]
    solve(sol, par, cu, group, gkv, gcu)

    for c in x_copies:
        c.wait()

    def corrections(f, carry):
        for i, x, sign in ((0, 0, 1.0), (1, XD - 1, -1.0)):
            rows = pl.ds(f * ROWS + x, LEV, stride=XD)
            tn[rows, :] += (sign * STEP_SIZE * PENALTY) * wp[0, x] * xr[i, f].astype(F32)
        return carry

    lax.fori_loop(0, FIELDS, corrections, 0)
    top = TOP * ROWS
    pre[...] = sol[:top, :] + tn[:top, :]
    for x in range(XD):
        vap[x] = sol[pl.ds(ROWS + x, LEV, stride=XD), :]
    rest[...] = (sol[top:, :] + tn[top:, :]).astype(BF16)
    couple(phys, mask, group)
    for k in order:
        message(k, 1).wait()


def solve(sol, par, cu, group, gkv, gcu):
    def forward(k, carry):
        kv_t, cu_t, kv_g, cu_g, prev, prev_g = carry
        here = par[pl.ds(k, XD, stride=LEV), :]
        inv = 1.0 / (1.0 + here + kv_t - kv_t * cu_t)
        low = kv_t * inv
        cu_t = here * inv
        at = pl.multiple_of(k * XD, XD)
        cu[pl.ds(at, XD), :] = cu_t
        values = []
        for f in range(FIELDS):
            rows = pl.ds(f * ROWS + at, XD)
            value = sol[rows, :] * inv + low * prev[f]
            sol[rows, :] = value
            values.append(value)
        here_g = gkv[pl.ds(k, 8, stride=LEV), :]
        inv_g = 1.0 / (1.0 + here_g + kv_g - kv_g * cu_g)
        low_g = kv_g * inv_g
        cu_g = here_g * inv_g
        gcu[pl.ds(pl.multiple_of(k * 8, 8), 8), :] = cu_g
        value_g = group[pl.ds(k, 8, stride=LEV), :] * inv_g + low_g * prev_g
        group[pl.ds(k, 8, stride=LEV), :] = value_g
        return here, cu_t, here_g, cu_g, tuple(values), value_g

    zt, zg = jnp.zeros((XD, YD), F32), jnp.zeros((8, 128), F32)
    lax.fori_loop(0, LEV, forward, (zt, zt, zg, zg, (zt,) * FIELDS, zg), unroll=4)

    def backward(i, carry):
        after, after_g = carry
        k = LEV - 1 - i
        at = pl.multiple_of(k * XD, XD)
        cu_t = cu[pl.ds(at, XD), :]
        values = []
        for f in range(FIELDS):
            rows = pl.ds(f * ROWS + at, XD)
            value = sol[rows, :] + cu_t * after[f]
            sol[rows, :] = value
            values.append(value)
        cu_g = gcu[pl.ds(pl.multiple_of(k * 8, 8), 8), :]
        value_g = group[pl.ds(k, 8, stride=LEV), :] + cu_g * after_g
        group[pl.ds(k, 8, stride=LEV), :] = value_g
        return tuple(values), value_g

    lax.fori_loop(0, LEV, backward, ((zt,) * FIELDS, zg), unroll=4)


def couple(phys, mask, group):
    for j in range(8):
        lanes = slice(j * 128, (j + 1) * 128)
        warm, ice = rates(phys[0, :, lanes], phys[1, :, lanes], mask[:, lanes])
        inv = 1.0 / (1.0 + warm + ice)
        passes = group[j * LEV : (j + 1) * LEV, :] * (inv + inv * inv)
        warm, ice = warm * passes, ice * passes
        for f in range(PF):
            phys[f, :, lanes] += COUPLE_WARM[f] * warm + COUPLE_ICE[f] * ice


def update_kernel(recv_b, hot, pre, vap, rest, phys, new_h, phys_h, fin, new, sems):
    top = TOP * ROWS
    copies = [
        pltpu.make_async_copy(rest, new_h.at[pl.ds(top, ALL_ROWS - top)], sems.at[0]),
        pltpu.make_async_copy(phys, phys_h, sems.at[2]),
    ]
    for c in copies:
        c.start()
    warms = t_dot(recv_b[:, 0].reshape(SLOTS, LEV), hot[...])
    ices = t_dot(recv_b[:, 1].reshape(SLOTS, LEV), hot[...])
    for x in range(XD):
        warm, ice = warms[:, x * YD : (x + 1) * YD], ices[:, x * YD : (x + 1) * YD]
        inv = 1.0 / (1.0 + warm + ice)
        rows = [pl.ds(f * ROWS + x, LEV, stride=XD) for f in range(TOP)]
        passes = vap[x] * (inv + inv * inv)
        to_warm, to_ice = warm * passes, ice * passes
        fin[rows[0], :] = pre[rows[0], :] + LATENT_WARM * to_warm + LATENT_ICE * to_ice
        fin[rows[1], :] = pre[rows[1], :] - (to_warm + to_ice)
        fin[rows[2], :] = pre[rows[2], :] + to_warm
        fin[rows[3], :] = pre[rows[3], :] + to_ice
    new[...] = fin[...].astype(BF16)
    copy = pltpu.make_async_copy(new, new_h.at[pl.ds(0, top)], sems.at[1])
    copy.start()
    copies.append(copy)
    for c in copies:
        c.wait()


def shards(atmos_state, horiz_wind, route_map, diffusivity, branch_mask, phys_state):
    q = atmos_state.reshape(ALL_ROWS, YD)
    wind = horiz_wind.reshape(2, ROWS, YD)
    const = jnp.asarray(constants())
    hbm = pl.BlockSpec(memory_space=pltpu.HBM)
    whole = pl.BlockSpec(memory_space=pltpu.VMEM)
    top = TOP * ROWS
    state = pl.pallas_call(
        exchange_kernel,
        out_shape=(
            pltpu.VMEM((COLS, 2, CAP, LEV), BF16),
            pltpu.VMEM((SLOTS, ROWS), BF16),
            pltpu.VMEM((top, YD), F32),
            pltpu.VMEM((XD, LEV, YD), F32),
            pltpu.VMEM((ALL_ROWS - top, YD), BF16),
            pltpu.VMEM((PF, LEV, SLOTS), F32),
        ),
        in_specs=[hbm] * 7,
        out_specs=(whole,) * 6,
        scratch_shapes=[
            pltpu.VMEM((ALL_ROWS, YD), BF16),
            pltpu.VMEM((XD, YD), jnp.int32),
            pltpu.VMEM((LEV, SLOTS), F32),
            pltpu.VMEM((LEV, SLOTS), jnp.int32),
            pltpu.VMEM((2, ROWS, YD), F32),
            pltpu.VMEM((384, 256), BF16),
            pltpu.VMEM((SLOTS, LEV), F32),
            pltpu.SemaphoreType.DMA((7,)),
            pltpu.VMEM((COLS, 2, CAP, LEV), BF16),
            pltpu.VMEM((COLS, 2, CAP, LEV), BF16),
            pltpu.VMEM((COLS, 2, CAP, LEV), BF16),
            pltpu.VMEM((ALL_ROWS, YD), F32),
            pltpu.VMEM((FIELDS, XD, LEV, YD), BF16),
            pltpu.VMEM((ALL_ROWS, YD), F32),
            pltpu.VMEM((2, FIELDS, LEV, YD), BF16),
            pltpu.VMEM((2 * YPAD, ROWS), BF16),
            pltpu.VMEM((2 * YPAD, ROWS), BF16),
            pltpu.VMEM((2, XD, LEV, YD), F32),
            pltpu.VMEM((XD * LEV, YD), F32),
            pltpu.VMEM((ROWS, YD), F32),
            pltpu.VMEM((8 * LEV, 128), F32),
            pltpu.VMEM((8 * LEV, 128), F32),
            pltpu.SemaphoreType.DMA((2, COLS)),
            pltpu.SemaphoreType.DMA((2, COLS)),
            pltpu.SemaphoreType.DMA((4,)),
            pltpu.SemaphoreType.DMA((4,)),
        ],
        compiler_params=pltpu.CompilerParams(
            collective_id=0, has_side_effects=True, vmem_limit_bytes=54 << 20
        ),
    )(q, route_map, diffusivity, branch_mask, phys_state, wind, const)
    new, phys_next = pl.pallas_call(
        update_kernel,
        out_shape=(
            jax.ShapeDtypeStruct((ALL_ROWS, YD), BF16),
            jax.ShapeDtypeStruct((PF, LEV, SLOTS), F32),
        ),
        in_specs=[whole] * 6,
        out_specs=(hbm,) * 2,
        scratch_shapes=[
            pltpu.VMEM((top, YD), F32),
            pltpu.VMEM((top, YD), BF16),
            pltpu.SemaphoreType.DMA((3,)),
        ],
        compiler_params=pltpu.CompilerParams(vmem_limit_bytes=32 << 20),
    )(*state)
    return new.reshape(FIELDS, LEV, XD, YD), phys_next


def solution(mesh):
    return jax.shard_map(
        shards,
        mesh=mesh,
        in_specs=(
            P(None, None, "edge", "cols"),
            P(None, None, "edge", "cols"),
            P("edge", "cols"),
            P(None, ("edge", "cols")),
            P(None, ("edge", "cols")),
            P(None, None, ("edge", "cols")),
        ),
        out_specs=(P(None, None, "edge", "cols"), P(None, None, ("edge", "cols"))),
        check_vma=False,
    )
```

```python
import functools

import jax
import jax.numpy as jnp
import numpy as np
from jax import lax
from jax.experimental import pallas as pl
from jax.experimental.pallas import tpu as pltpu
from jax.sharding import PartitionSpec as P

MESH = pl.DeviceIdType.MESH
F32, BF16 = jnp.float32, jnp.bfloat16
FIELDS, LEV, XD, YD = 11, 128, 4, 128
EDGE, COLS, CAP, PF = 4, 32, 32, 8
SLOTS = COLS * CAP
ROWS = LEV * XD
ALL_ROWS = FIELDS * ROWS
TOP = 4
YPAD = 16
PENALTY = 3.0
STEP_SIZE = 0.05
LATENT_WARM = 0.5
LATENT_ICE = 0.6
COUPLE_WARM = [0.8, -0.6, 0.5, 0.9, -0.7, 0.4, 1.0, -0.5]
COUPLE_ICE = [-0.4, 0.7, 0.9, -0.5, 0.6, -0.8, 0.3, 0.7]


def gll_matrix():
    nodes = np.array([-1.0, -1.0 / np.sqrt(5.0), 1.0 / np.sqrt(5.0), 1.0])
    prod = [np.prod([nodes[i] - nodes[j] for j in range(4) if j != i]) for i in range(4)]
    table = np.zeros((4, 4))
    for i in range(4):
        for j in range(4):
            if i != j:
                table[i, j] = prod[i] / (prod[j] * (nodes[i] - nodes[j]))
            else:
                table[i, i] = sum(1.0 / (nodes[i] - nodes[k]) for k in range(4) if k != i)
    return table


def split_bf16(table):
    high = table.astype(np.float32).astype(BF16)
    low = (table - high.astype(np.float64)).astype(np.float32).astype(BF16)
    return high, low


def derivative():
    own = gll_matrix()
    own[0, 0] += PENALTY
    own[3, 3] -= PENALTY
    return -STEP_SIZE * own


def constants():
    own = derivative() / -STEP_SIZE
    gy = np.zeros((YD, YD))
    for el in range(YD // 4):
        gy[4 * el : 4 * el + 4, 4 * el : 4 * el + 4] = own.T
        if el:
            gy[4 * el - 1, 4 * el] = -PENALTY
        if el < YD // 4 - 1:
            gy[4 * el + 4, 4 * el + 3] = PENALTY
    ey = np.zeros((YD, YD))
    ey[:YPAD, 0] = -PENALTY
    ey[YPAD : 2 * YPAD, YD - 1] = PENALTY
    table = np.concatenate(split_bf16(-STEP_SIZE * np.concatenate([gy, ey], 0)), 1)
    tri = np.triu(np.ones((YD, YD)), 1)
    square = np.concatenate([tri, np.eye(128)], 1).astype(BF16)
    return np.concatenate([table, square], 0)


def far_first():
    def dist(k):
        z, y = k // 8, (k // 2) % 4
        return min(z, 4 - z) + min(y, 4 - y)

    return sorted(range(1, COLS), key=lambda k: -dist(k))


def softplus(x):
    return jnp.maximum(x, 0.0) + jnp.log1p(jnp.exp(-jnp.abs(x)))


def rates(phys0, phys1, mask):
    warm = jnp.where((mask & 1) == 1, softplus(phys0), 0.0)
    ice = jnp.where(mask >= 2, softplus(phys1), 0.0)
    return warm, ice


def dot(a, b):
    return jnp.dot(a, b, preferred_element_type=F32)


def dot_t(a, b):
    return lax.dot_general(a, b, (((1,), (1,)), ((), ())), preferred_element_type=F32)


def t_dot(a, b):
    return lax.dot_general(a, b, (((0,), (0,)), ((), ())), preferred_element_type=F32)


def exchange_kernel(
    q_h, route_h, kv_h, mask_h, phys_h, wind_h, const_h,
    recv_b, hot, pre, vap, rest, phys,
    qv, route, kv, mask, wind, const, group, gain, in_sem,
    snd_a, snd_b, recv_a, sol, qp, tn, xr, ys, yr, wp, par, cu, gkv, gcu,
    ss, rs, hss, hrs,
):
    e, me = lax.axis_index("edge"), lax.axis_index("cols")
    core, yy, zz = me % 2, (me // 2) % 4, me // 8
    order = far_first()

    def peer(k):
        return ((zz + k // 8) % 4) * 8 + ((yy + (k // 2) % 4) % 4) * 2 + (core + k % 2) % 2

    up_x, down_x = (e + 1) % EDGE, (e + EDGE - 1) % EDGE
    up_y, down_y = (me + 1) % COLS, (me + COLS - 1) % COLS
    loads = [
        pltpu.make_async_copy(a, b, in_sem.at[i])
        for i, (a, b) in enumerate(
            (
                (const_h, const), (kv_h, kv), (route_h, route), (q_h, qv),
                (mask_h, mask), (phys_h.at[pl.ds(0, 2)], phys.at[pl.ds(0, 2)]), (wind_h, wind),
                (phys_h.at[pl.ds(2, PF - 2)], phys.at[pl.ds(2, PF - 2)]),
            )
        )
    ]
    for c in loads[:4]:
        c.start()
    bar = pltpu.get_barrier_semaphore()
    for k in order:
        pl.semaphore_signal(bar, inc=1, device_id=(e, peer(k)), device_id_type=MESH)
    for to in (up_x, down_x):
        pl.semaphore_signal(bar, inc=1, device_id=(to, me), device_id_type=MESH)
    tri = const.at[pl.ds(256, 128), pl.ds(0, 128)]
    eye = const.at[pl.ds(256, 128), pl.ds(128, 128)]

    def turn(j, value):
        turned = dot_t(eye[...], value.astype(BF16)).astype(BF16)
        return turned.reshape(4, CAP, LEV)

    loads[0].wait()
    loads[1].wait()
    for c in loads[4:7]:
        c.start()
    for j in range(8):
        coupling = kv[:, j * 128 : (j + 1) * 128]
        snd_a[4 * j : 4 * j + 4, 0] = turn(j, coupling)
        gkv[pl.ds(j, LEV, stride=8), :] = coupling

    loads[2].wait()
    dest_at = lax.broadcasted_iota(jnp.int32, (COLS, YD), 0)
    slot_at = lax.broadcasted_iota(jnp.int32, (SLOTS, YD), 0)
    before = jnp.zeros((COLS, 1), F32)
    for x in range(XD):
        chosen = dest_at == route[x : x + 1, :]
        chosen_f = jnp.where(chosen, 1.0, 0.0)
        earlier = dot(chosen_f.astype(BF16), tri[...]) + before
        before = before + jnp.sum(chosen_f, axis=1, keepdims=True)
        rank = jnp.sum(jnp.where(chosen, earlier, 0.0), axis=0, keepdims=True)
        slots = route[x : x + 1, :] * CAP + rank.astype(jnp.int32)
        hot[:, x * YD : (x + 1) * YD] = jnp.where(slot_at == slots, 1.0, 0.0).astype(BF16)

    loads[3].wait()

    def planes(f, carry):
        rows = pl.ds(pl.multiple_of(f * ROWS, ROWS), ROWS)
        sol[rows, :] = qv[rows, :].astype(F32)
        for x in range(XD):
            qp[f, x] = sol[pl.ds(f * ROWS + x, LEV, stride=XD), :].astype(BF16)
        return carry

    lax.fori_loop(0, FIELDS, planes, 0)
    total = dot_t(hot[...], jnp.concatenate([qp[1, x] for x in range(XD)], axis=1))
    snd_a[:, 1] = total.astype(BF16).reshape(COLS, CAP, LEV)

    fields = jnp.concatenate([qp[f].reshape(ROWS, YD) for f in range(FIELDS)], axis=1)
    at = lax.broadcasted_iota(jnp.int32, (YD, YD), 0)
    lane = lax.broadcasted_iota(jnp.int32, (YD, YD), 1)
    pick = [
        jnp.where(((at == 0) & (lane == f)) | ((at == YD - 1) & (lane == YPAD + f)), 1.0, 0.0)
        for f in range(FIELDS)
    ]
    ends = dot(fields, jnp.concatenate(pick, axis=0).astype(BF16)).astype(BF16)
    ys[...] = dot_t(eye[0 : 2 * YPAD, :], ends).astype(BF16)

    pl.semaphore_wait(bar, COLS - 1 + 2)
    y_copies, x_copies = [], []
    for i, to in ((0, down_y), (1, up_y)):
        y_copies.append(
            pltpu.make_async_remote_copy(
                ys.at[pl.ds(i * YPAD, YPAD)], yr.at[pl.ds((1 - i) * YPAD, YPAD)],
                hss.at[2 + i], hrs.at[3 - i],
                device_id=(e, to), device_id_type=MESH,
            )
        )
    for i, to in ((0, down_x), (1, up_x)):
        x_copies.append(
            pltpu.make_async_remote_copy(
                qp.at[:, i * (XD - 1)], xr.at[1 - i], hss.at[i], hrs.at[1 - i],
                device_id=(to, me), device_id_type=MESH,
            )
        )
    for c in y_copies + x_copies:
        c.start()

    def message(k, part):
        to = peer(k)
        source, target = ((snd_a, recv_a), (snd_b, recv_b))[part]
        return pltpu.make_async_remote_copy(
            source.at[to], target.at[me], ss.at[part, k], rs.at[part, k],
            device_id=(e, to), device_id_type=MESH,
        )

    for k in order:
        message(k, 0).start()
    loads[4].wait()
    loads[5].wait()
    for j in range(8):
        lanes = slice(j * 128, (j + 1) * 128)
        warm, ice = rates(phys[0, :, lanes], phys[1, :, lanes], mask[:, lanes])
        inv = 1.0 / (1.0 + warm + ice)
        share = inv + inv * inv
        gain[0, :, lanes] = warm * share
        gain[1, :, lanes] = ice * share
        snd_b[4 * j : 4 * j + 4, 0] = turn(j, warm)
        snd_b[4 * j : 4 * j + 4, 1] = turn(j, ice)
    loads[7].start()
    recv_a[pl.ds(me, 1)] = snd_a[pl.ds(me, 1)]
    recv_b[pl.ds(me, 1)] = snd_b[pl.ds(me, 1)]

    loads[6].wait()
    for i in range(2):
        for x in range(XD):
            wp[i, x] = wind[i, pl.ds(x, LEV, stride=XD), :]
    for c in y_copies:
        c.wait()
    y_halo = t_dot(yr[...], eye[0 : 2 * YPAD, :])
    wide = lax.broadcasted_iota(jnp.int32, (ROWS, YD), 1)
    along = derivative()

    def dynamics(f, carry):
        near = jnp.where((wide == f) | (wide == YPAD + f), y_halo, 0.0).astype(BF16)
        both = jnp.concatenate([qp[f].reshape(ROWS, YD), near], axis=1)
        dy = dot(both, const[0:256, :])
        own = [qp[f, x].astype(F32) for x in range(XD)]
        for x in range(XD):
            dx = sum(float(along[x, i]) * own[i] for i in range(XD) if abs(along[x, i]) > 1e-9)
            rows = slice(x * LEV, (x + 1) * LEV)
            tn[pl.ds(f * ROWS + x, LEV, stride=XD), :] = wp[0, x] * dx + wp[1, x] * (
                dy[rows, :YD] + dy[rows, YD:]
            )
        return carry

    lax.fori_loop(0, FIELDS, dynamics, 0)
    for k in order:
        message(k, 1).start()

    for k in order:
        message(k, 0).wait()
    here = t_dot(recv_a[:, 0].reshape(SLOTS, LEV), hot[...])
    for x in range(XD):
        par[x * LEV : (x + 1) * LEV, :] = here[:, x * YD : (x + 1) * YD]
    for j in range(8):
        vapour = recv_a[4 * j : 4 * j + 4, 1].reshape(128, LEV)
        group[pl.ds(j, LEV, stride=8), :] = dot_t(eye[...], vapour)
    solve(sol, par, cu, group, gkv, gcu)

    for c in x_copies:
        c.wait()

    def corrections(f, carry):
        for i, x, sign in ((0, 0, 1.0), (1, XD - 1, -1.0)):
            rows = pl.ds(f * ROWS + x, LEV, stride=XD)
            tn[rows, :] += (sign * STEP_SIZE * PENALTY) * wp[0, x] * xr[i, f].astype(F32)
        return carry

    lax.fori_loop(0, FIELDS, corrections, 0)
    top = TOP * ROWS
    pre[...] = sol[:top, :] + tn[:top, :]
    for x in range(XD):
        vap[x] = sol[pl.ds(ROWS + x, LEV, stride=XD), :]
    rest[...] = (sol[top:, :] + tn[top:, :]).astype(BF16)
    loads[7].wait()
    couple(phys, gain, group)
    for k in order:
        message(k, 1).wait()


def solve(sol, par, cu, group, gkv, gcu):
    def forward(k, carry):
        kv_t, cu_t, kv_g, cu_g, prev, prev_g = carry
        here = par[pl.ds(k, XD, stride=LEV), :]
        inv = 1.0 / (1.0 + here + kv_t - kv_t * cu_t)
        low = kv_t * inv
        cu_t = here * inv
        at = pl.multiple_of(k * XD, XD)
        cu[pl.ds(at, XD), :] = cu_t
        values = []
        for f in range(FIELDS):
            rows = pl.ds(f * ROWS + at, XD)
            value = sol[rows, :] * inv + low * prev[f]
            sol[rows, :] = value
            values.append(value)
        at8 = pl.ds(pl.multiple_of(k * 8, 8), 8)
        here_g = gkv[at8, :]
        inv_g = 1.0 / (1.0 + here_g + kv_g - kv_g * cu_g)
        low_g = kv_g * inv_g
        cu_g = here_g * inv_g
        gcu[at8, :] = cu_g
        value_g = group[at8, :] * inv_g + low_g * prev_g
        group[at8, :] = value_g
        return here, cu_t, here_g, cu_g, tuple(values), value_g

    zt, zg = jnp.zeros((XD, YD), F32), jnp.zeros((8, 128), F32)
    lax.fori_loop(0, LEV, forward, (zt, zt, zg, zg, (zt,) * FIELDS, zg), unroll=16)

    def backward(i, carry):
        after, after_g = carry
        k = LEV - 1 - i
        at = pl.multiple_of(k * XD, XD)
        cu_t = cu[pl.ds(at, XD), :]
        values = []
        for f in range(FIELDS):
            rows = pl.ds(f * ROWS + at, XD)
            value = sol[rows, :] + cu_t * after[f]
            sol[rows, :] = value
            values.append(value)
        at8 = pl.ds(pl.multiple_of(k * 8, 8), 8)
        value_g = group[at8, :] + gcu[at8, :] * after_g
        group[at8, :] = value_g
        return tuple(values), value_g

    lax.fori_loop(0, LEV, backward, ((zt,) * FIELDS, zg), unroll=16)


def couple(phys, gain, group):
    for j in range(8):
        lanes = slice(j * 128, (j + 1) * 128)
        vapour = group[pl.ds(j, LEV, stride=8), :]
        warm, ice = gain[0, :, lanes] * vapour, gain[1, :, lanes] * vapour
        for f in range(PF):
            phys[f, :, lanes] += COUPLE_WARM[f] * warm + COUPLE_ICE[f] * ice


def update_kernel(recv_b, hot, pre, vap, rest, phys, new_h, phys_h, fin, new, sems):
    top = TOP * ROWS
    copies = [
        pltpu.make_async_copy(rest, new_h.at[pl.ds(top, ALL_ROWS - top)], sems.at[0]),
        pltpu.make_async_copy(phys, phys_h, sems.at[2]),
    ]
    for c in copies:
        c.start()
    warms = t_dot(recv_b[:, 0].reshape(SLOTS, LEV), hot[...])
    ices = t_dot(recv_b[:, 1].reshape(SLOTS, LEV), hot[...])
    for x in range(XD):
        warm, ice = warms[:, x * YD : (x + 1) * YD], ices[:, x * YD : (x + 1) * YD]
        inv = 1.0 / (1.0 + warm + ice)
        rows = [pl.ds(f * ROWS + x, LEV, stride=XD) for f in range(TOP)]
        passes = vap[x] * (inv + inv * inv)
        to_warm, to_ice = warm * passes, ice * passes
        fin[rows[0], :] = pre[rows[0], :] + LATENT_WARM * to_warm + LATENT_ICE * to_ice
        fin[rows[1], :] = pre[rows[1], :] - (to_warm + to_ice)
        fin[rows[2], :] = pre[rows[2], :] + to_warm
        fin[rows[3], :] = pre[rows[3], :] + to_ice
    new[...] = fin[...].astype(BF16)
    copy = pltpu.make_async_copy(new, new_h.at[pl.ds(0, top)], sems.at[1])
    copy.start()
    copies.append(copy)
    for c in copies:
        c.wait()


def shards(atmos_state, horiz_wind, route_map, diffusivity, branch_mask, phys_state):
    q = atmos_state.reshape(ALL_ROWS, YD)
    wind = horiz_wind.reshape(2, ROWS, YD)
    const = jnp.asarray(constants())
    hbm = pl.BlockSpec(memory_space=pltpu.HBM)
    whole = pl.BlockSpec(memory_space=pltpu.VMEM)
    top = TOP * ROWS
    state = pl.pallas_call(
        exchange_kernel,
        out_shape=(
            pltpu.VMEM((COLS, 2, CAP, LEV), BF16),
            pltpu.VMEM((SLOTS, ROWS), BF16),
            pltpu.VMEM((top, YD), F32),
            pltpu.VMEM((XD, LEV, YD), F32),
            pltpu.VMEM((ALL_ROWS - top, YD), BF16),
            pltpu.VMEM((PF, LEV, SLOTS), F32),
        ),
        in_specs=[hbm] * 7,
        out_specs=(whole,) * 6,
        scratch_shapes=[
            pltpu.VMEM((ALL_ROWS, YD), BF16),
            pltpu.VMEM((XD, YD), jnp.int32),
            pltpu.VMEM((LEV, SLOTS), F32),
            pltpu.VMEM((LEV, SLOTS), jnp.int32),
            pltpu.VMEM((2, ROWS, YD), F32),
            pltpu.VMEM((384, 256), BF16),
            pltpu.VMEM((SLOTS, LEV), F32),
            pltpu.VMEM((2, LEV, SLOTS), F32),
            pltpu.SemaphoreType.DMA((8,)),
            pltpu.VMEM((COLS, 2, CAP, LEV), BF16),
            pltpu.VMEM((COLS, 2, CAP, LEV), BF16),
            pltpu.VMEM((COLS, 2, CAP, LEV), BF16),
            pltpu.VMEM((ALL_ROWS, YD), F32),
            pltpu.VMEM((FIELDS, XD, LEV, YD), BF16),
            pltpu.VMEM((ALL_ROWS, YD), F32),
            pltpu.VMEM((2, FIELDS, LEV, YD), BF16),
            pltpu.VMEM((2 * YPAD, ROWS), BF16),
            pltpu.VMEM((2 * YPAD, ROWS), BF16),
            pltpu.VMEM((2, XD, LEV, YD), F32),
            pltpu.VMEM((XD * LEV, YD), F32),
            pltpu.VMEM((ROWS, YD), F32),
            pltpu.VMEM((8 * LEV, 128), F32),
            pltpu.VMEM((8 * LEV, 128), F32),
            pltpu.SemaphoreType.DMA((2, COLS)),
            pltpu.SemaphoreType.DMA((2, COLS)),
            pltpu.SemaphoreType.DMA((4,)),
            pltpu.SemaphoreType.DMA((4,)),
        ],
        compiler_params=pltpu.CompilerParams(
            collective_id=0, has_side_effects=True, vmem_limit_bytes=54 << 20
        ),
    )(q, route_map, diffusivity, branch_mask, phys_state, wind, const)
    new, phys_next = pl.pallas_call(
        update_kernel,
        out_shape=(
            jax.ShapeDtypeStruct((ALL_ROWS, YD), BF16),
            jax.ShapeDtypeStruct((PF, LEV, SLOTS), F32),
        ),
        in_specs=[whole] * 6,
        out_specs=(hbm,) * 2,
        scratch_shapes=[
            pltpu.VMEM((top, YD), F32),
            pltpu.VMEM((top, YD), BF16),
            pltpu.SemaphoreType.DMA((3,)),
        ],
        compiler_params=pltpu.CompilerParams(vmem_limit_bytes=32 << 20),
    )(*state)
    return new.reshape(FIELDS, LEV, XD, YD), phys_next


def solution(mesh):
    return jax.shard_map(
        shards,
        mesh=mesh,
        in_specs=(
            P(None, None, "edge", "cols"),
            P(None, None, "edge", "cols"),
            P("edge", "cols"),
            P(None, ("edge", "cols")),
            P(None, ("edge", "cols")),
            P(None, None, ("edge", "cols")),
        ),
        out_specs=(P(None, None, "edge", "cols"), P(None, None, ("edge", "cols"))),
        check_vma=False,
    )
```

```python
import functools

import jax
import jax.numpy as jnp
import numpy as np
from jax import lax
from jax.experimental import pallas as pl
from jax.experimental.pallas import tpu as pltpu
from jax.sharding import PartitionSpec as P

MESH = pl.DeviceIdType.MESH
F32, BF16 = jnp.float32, jnp.bfloat16
FIELDS, LEV, XD, YD = 11, 128, 4, 128
EDGE, COLS, CAP, PF = 4, 32, 32, 8
SLOTS = COLS * CAP
ROWS = LEV * XD
ALL_ROWS = FIELDS * ROWS
TOP = 4
YPAD = 16
PENALTY = 3.0
STEP_SIZE = 0.05
LATENT_WARM = 0.5
LATENT_ICE = 0.6
COUPLE_WARM = [0.8, -0.6, 0.5, 0.9, -0.7, 0.4, 1.0, -0.5]
COUPLE_ICE = [-0.4, 0.7, 0.9, -0.5, 0.6, -0.8, 0.3, 0.7]


def gll_matrix():
    nodes = np.array([-1.0, -1.0 / np.sqrt(5.0), 1.0 / np.sqrt(5.0), 1.0])
    prod = [np.prod([nodes[i] - nodes[j] for j in range(4) if j != i]) for i in range(4)]
    table = np.zeros((4, 4))
    for i in range(4):
        for j in range(4):
            if i != j:
                table[i, j] = prod[i] / (prod[j] * (nodes[i] - nodes[j]))
            else:
                table[i, i] = sum(1.0 / (nodes[i] - nodes[k]) for k in range(4) if k != i)
    return table


def split_bf16(table):
    high = table.astype(np.float32).astype(BF16)
    low = (table - high.astype(np.float64)).astype(np.float32).astype(BF16)
    return high, low


def derivative():
    own = gll_matrix()
    own[0, 0] += PENALTY
    own[3, 3] -= PENALTY
    return -STEP_SIZE * own


def constants():
    own = derivative() / -STEP_SIZE
    gy = np.zeros((YD, YD))
    for el in range(YD // 4):
        gy[4 * el : 4 * el + 4, 4 * el : 4 * el + 4] = own.T
        if el:
            gy[4 * el - 1, 4 * el] = -PENALTY
        if el < YD // 4 - 1:
            gy[4 * el + 4, 4 * el + 3] = PENALTY
    ey = np.zeros((YD, YD))
    ey[:YPAD, 0] = -PENALTY
    ey[YPAD : 2 * YPAD, YD - 1] = PENALTY
    table = np.concatenate(split_bf16(-STEP_SIZE * np.concatenate([gy, ey], 0)), 1)
    tri = np.triu(np.ones((YD, YD)), 1)
    square = np.concatenate([tri, np.eye(128)], 1).astype(BF16)
    return np.concatenate([table, square], 0)


def far_first():
    def dist(k):
        z, y = k // 8, (k // 2) % 4
        return min(z, 4 - z) + min(y, 4 - y)

    return sorted(range(1, COLS), key=lambda k: -dist(k))


def softplus(x):
    return jnp.maximum(x, 0.0) + jnp.log1p(jnp.exp(-jnp.abs(x)))


def rates(phys0, phys1, mask):
    warm = jnp.where((mask & 1) == 1, softplus(phys0), 0.0)
    ice = jnp.where(mask >= 2, softplus(phys1), 0.0)
    return warm, ice


def dot(a, b):
    return jnp.dot(a, b, preferred_element_type=F32)


def dot_t(a, b):
    return lax.dot_general(a, b, (((1,), (1,)), ((), ())), preferred_element_type=F32)


def t_dot(a, b):
    return lax.dot_general(a, b, (((0,), (0,)), ((), ())), preferred_element_type=F32)


def exchange_kernel(
    q_h, route_h, kv_h, mask_h, phys_h, wind_h, const_h,
    recv_b, hot, pre, vap, rest, phys,
    qv, route, kv, mask, wind, const, group, gain, in_sem,
    snd_a, snd_b, recv_a, sol, qp, tn, xr, ys, yr, wp, par, cu, gkv, gcu,
    ss, rs, hss, hrs,
):
    e, me = lax.axis_index("edge"), lax.axis_index("cols")
    core, yy, zz = me % 2, (me // 2) % 4, me // 8
    order = far_first()

    def peer(k):
        return ((zz + k // 8) % 4) * 8 + ((yy + (k // 2) % 4) % 4) * 2 + (core + k % 2) % 2

    up_x, down_x = (e + 1) % EDGE, (e + EDGE - 1) % EDGE
    up_y, down_y = (me + 1) % COLS, (me + COLS - 1) % COLS
    loads = [
        pltpu.make_async_copy(a, b, in_sem.at[i])
        for i, (a, b) in enumerate(
            (
                (const_h, const), (kv_h, kv), (route_h, route), (q_h, qv),
                (mask_h, mask), (phys_h.at[pl.ds(0, 2)], phys.at[pl.ds(0, 2)]), (wind_h, wind),
                (phys_h.at[pl.ds(2, PF - 2)], phys.at[pl.ds(2, PF - 2)]),
            )
        )
    ]
    for c in loads[:4]:
        c.start()
    bar = pltpu.get_barrier_semaphore()
    for k in order:
        pl.semaphore_signal(bar, inc=1, device_id=(e, peer(k)), device_id_type=MESH)
    for to in (up_x, down_x):
        pl.semaphore_signal(bar, inc=1, device_id=(to, me), device_id_type=MESH)
    tri = const.at[pl.ds(256, 128), pl.ds(0, 128)]
    eye = const.at[pl.ds(256, 128), pl.ds(128, 128)]

    def turn(j, value):
        turned = dot_t(eye[...], value.astype(BF16)).astype(BF16)
        return turned.reshape(4, CAP, LEV)

    loads[0].wait()
    loads[1].wait()
    for c in loads[4:7]:
        c.start()
    for j in range(8):
        coupling = kv[:, j * 128 : (j + 1) * 128]
        snd_a[4 * j : 4 * j + 4, 0] = turn(j, coupling)
        gkv[pl.ds(j, LEV, stride=8), :] = coupling

    loads[2].wait()
    dest_at = lax.broadcasted_iota(jnp.int32, (COLS, YD), 0)
    slot_at = lax.broadcasted_iota(jnp.int32, (SLOTS, YD), 0)
    before = jnp.zeros((COLS, 1), F32)
    for x in range(XD):
        chosen = dest_at == route[x : x + 1, :]
        chosen_f = jnp.where(chosen, 1.0, 0.0)
        earlier = dot(chosen_f.astype(BF16), tri[...]) + before
        before = before + jnp.sum(chosen_f, axis=1, keepdims=True)
        rank = jnp.sum(jnp.where(chosen, earlier, 0.0), axis=0, keepdims=True)
        slots = route[x : x + 1, :] * CAP + rank.astype(jnp.int32)
        hot[:, x * YD : (x + 1) * YD] = jnp.where(slot_at == slots, 1.0, 0.0).astype(BF16)

    loads[3].wait()

    def planes(f, carry):
        rows = pl.ds(pl.multiple_of(f * ROWS, ROWS), ROWS)
        sol[rows, :] = qv[rows, :].astype(F32)
        for x in range(XD):
            qp[f, x] = sol[pl.ds(f * ROWS + x, LEV, stride=XD), :].astype(BF16)
        return carry

    lax.fori_loop(0, FIELDS, planes, 0)
    total = dot_t(hot[...], jnp.concatenate([qp[1, x] for x in range(XD)], axis=1))
    snd_a[:, 1] = total.astype(BF16).reshape(COLS, CAP, LEV)

    fields = jnp.concatenate([qp[f].reshape(ROWS, YD) for f in range(FIELDS)], axis=1)
    at = lax.broadcasted_iota(jnp.int32, (YD, YD), 0)
    lane = lax.broadcasted_iota(jnp.int32, (YD, YD), 1)
    pick = [
        jnp.where(((at == 0) & (lane == f)) | ((at == YD - 1) & (lane == YPAD + f)), 1.0, 0.0)
        for f in range(FIELDS)
    ]
    ends = dot(fields, jnp.concatenate(pick, axis=0).astype(BF16)).astype(BF16)
    ys[...] = dot_t(eye[0 : 2 * YPAD, :], ends).astype(BF16)

    pl.semaphore_wait(bar, COLS - 1 + 2)
    y_copies, x_copies = [], []
    for i, to in ((0, down_y), (1, up_y)):
        y_copies.append(
            pltpu.make_async_remote_copy(
                ys.at[pl.ds(i * YPAD, YPAD)], yr.at[pl.ds((1 - i) * YPAD, YPAD)],
                hss.at[2 + i], hrs.at[3 - i],
                device_id=(e, to), device_id_type=MESH,
            )
        )
    for i, to in ((0, down_x), (1, up_x)):
        x_copies.append(
            pltpu.make_async_remote_copy(
                qp.at[:, i * (XD - 1)], xr.at[1 - i], hss.at[i], hrs.at[1 - i],
                device_id=(to, me), device_id_type=MESH,
            )
        )
    for c in y_copies + x_copies:
        c.start()

    def message(k, part):
        to = peer(k)
        source, target = ((snd_a, recv_a), (snd_b, recv_b))[part]
        return pltpu.make_async_remote_copy(
            source.at[to], target.at[me], ss.at[part], rs.at[part],
            device_id=(e, to), device_id_type=MESH,
        )

    def settle(part):
        source, target = ((snd_a, recv_a), (snd_b, recv_b))[part]
        others = pl.ds(0, COLS - 1)
        pltpu.make_async_remote_copy(
            source.at[others], target.at[others], ss.at[part], rs.at[part],
            device_id=(e, peer(1)), device_id_type=MESH,
        ).wait()

    for k in order:
        message(k, 0).start()
    loads[4].wait()
    loads[5].wait()
    for j in range(8):
        lanes = slice(j * 128, (j + 1) * 128)
        warm, ice = rates(phys[0, :, lanes], phys[1, :, lanes], mask[:, lanes])
        inv = 1.0 / (1.0 + warm + ice)
        share = inv + inv * inv
        gain[0, :, lanes] = warm * share
        gain[1, :, lanes] = ice * share
        snd_b[4 * j : 4 * j + 4, 0] = turn(j, warm)
        snd_b[4 * j : 4 * j + 4, 1] = turn(j, ice)
    loads[7].start()
    recv_a[pl.ds(me, 1)] = snd_a[pl.ds(me, 1)]
    recv_b[pl.ds(me, 1)] = snd_b[pl.ds(me, 1)]

    loads[6].wait()
    for i in range(2):
        for x in range(XD):
            wp[i, x] = wind[i, pl.ds(x, LEV, stride=XD), :]
    for c in y_copies:
        c.wait()
    y_halo = t_dot(yr[...], eye[0 : 2 * YPAD, :])
    wide = lax.broadcasted_iota(jnp.int32, (ROWS, YD), 1)
    along = derivative()

    def dynamics(f, carry):
        near = jnp.where((wide == f) | (wide == YPAD + f), y_halo, 0.0).astype(BF16)
        both = jnp.concatenate([qp[f].reshape(ROWS, YD), near], axis=1)
        dy = dot(both, const[0:256, :])
        own = [qp[f, x].astype(F32) for x in range(XD)]
        for x in range(XD):
            dx = sum(float(along[x, i]) * own[i] for i in range(XD) if abs(along[x, i]) > 1e-9)
            rows = slice(x * LEV, (x + 1) * LEV)
            tn[pl.ds(f * ROWS + x, LEV, stride=XD), :] = wp[0, x] * dx + wp[1, x] * (
                dy[rows, :YD] + dy[rows, YD:]
            )
        return carry

    lax.fori_loop(0, FIELDS, dynamics, 0)
    for k in order:
        message(k, 1).start()

    settle(0)
    here = t_dot(recv_a[:, 0].reshape(SLOTS, LEV), hot[...])
    for x in range(XD):
        par[x * LEV : (x + 1) * LEV, :] = here[:, x * YD : (x + 1) * YD]
    for j in range(8):
        vapour = recv_a[4 * j : 4 * j + 4, 1].reshape(128, LEV)
        group[pl.ds(j, LEV, stride=8), :] = dot_t(eye[...], vapour)
    solve(sol, par, cu, group, gkv, gcu)

    loads[7].wait()
    couple(phys, gain, group)
    for c in x_copies:
        c.wait()

    def corrections(f, carry):
        for i, x, sign in ((0, 0, 1.0), (1, XD - 1, -1.0)):
            rows = pl.ds(f * ROWS + x, LEV, stride=XD)
            tn[rows, :] += (sign * STEP_SIZE * PENALTY) * wp[0, x] * xr[i, f].astype(F32)
        return carry

    lax.fori_loop(0, FIELDS, corrections, 0)
    top = TOP * ROWS
    pre[...] = sol[:top, :] + tn[:top, :]
    for x in range(XD):
        vap[x] = sol[pl.ds(ROWS + x, LEV, stride=XD), :]
    rest[...] = (sol[top:, :] + tn[top:, :]).astype(BF16)
    settle(1)


def solve(sol, par, cu, group, gkv, gcu):
    def forward(k, carry):
        kv_t, cu_t, kv_g, cu_g, prev, prev_g = carry
        here = par[pl.ds(k, XD, stride=LEV), :]
        inv = 1.0 / (1.0 + here + kv_t - kv_t * cu_t)
        low = kv_t * inv
        cu_t = here * inv
        at = pl.multiple_of(k * XD, XD)
        cu[pl.ds(at, XD), :] = cu_t
        values = []
        for f in range(FIELDS):
            rows = pl.ds(f * ROWS + at, XD)
            value = sol[rows, :] * inv + low * prev[f]
            sol[rows, :] = value
            values.append(value)
        at8 = pl.ds(pl.multiple_of(k * 8, 8), 8)
        here_g = gkv[at8, :]
        inv_g = 1.0 / (1.0 + here_g + kv_g - kv_g * cu_g)
        low_g = kv_g * inv_g
        cu_g = here_g * inv_g
        gcu[at8, :] = cu_g
        value_g = group[at8, :] * inv_g + low_g * prev_g
        group[at8, :] = value_g
        return here, cu_t, here_g, cu_g, tuple(values), value_g

    zt, zg = jnp.zeros((XD, YD), F32), jnp.zeros((8, 128), F32)
    lax.fori_loop(0, LEV, forward, (zt, zt, zg, zg, (zt,) * FIELDS, zg), unroll=16)

    def backward(i, carry):
        after, after_g = carry
        k = LEV - 1 - i
        at = pl.multiple_of(k * XD, XD)
        cu_t = cu[pl.ds(at, XD), :]
        values = []
        for f in range(FIELDS):
            rows = pl.ds(f * ROWS + at, XD)
            value = sol[rows, :] + cu_t * after[f]
            sol[rows, :] = value
            values.append(value)
        at8 = pl.ds(pl.multiple_of(k * 8, 8), 8)
        value_g = group[at8, :] + gcu[at8, :] * after_g
        group[at8, :] = value_g
        return tuple(values), value_g

    lax.fori_loop(0, LEV, backward, ((zt,) * FIELDS, zg), unroll=16)


def couple(phys, gain, group):
    for j in range(8):
        lanes = slice(j * 128, (j + 1) * 128)
        vapour = group[pl.ds(j, LEV, stride=8), :]
        warm, ice = gain[0, :, lanes] * vapour, gain[1, :, lanes] * vapour
        for f in range(PF):
            phys[f, :, lanes] += COUPLE_WARM[f] * warm + COUPLE_ICE[f] * ice


def update_kernel(recv_b, hot, pre, vap, rest, phys, new_h, phys_h, fin, new, sems):
    top = TOP * ROWS
    copies = [
        pltpu.make_async_copy(rest, new_h.at[pl.ds(top, ALL_ROWS - top)], sems.at[0]),
        pltpu.make_async_copy(phys, phys_h, sems.at[2]),
    ]
    for c in copies:
        c.start()
    both = jnp.concatenate([recv_b[:, i].reshape(SLOTS, LEV) for i in range(2)], axis=1)
    both = t_dot(both, hot[...])
    for x in range(XD):
        warm, ice = both[:LEV, x * YD : (x + 1) * YD], both[LEV:, x * YD : (x + 1) * YD]
        inv = 1.0 / (1.0 + warm + ice)
        passes = vap[x] * (inv + inv * inv)
        warm, ice = warm * passes, ice * passes
        gains = (LATENT_WARM * warm + LATENT_ICE * ice, -(warm + ice), warm, ice)
        for f in range(TOP):
            rows = pl.ds(f * ROWS + x, LEV, stride=XD)
            fin[rows, :] = pre[rows, :] + gains[f]
    for f in range(TOP):
        rows = pl.ds(f * ROWS, ROWS)
        new[rows, :] = fin[rows, :].astype(BF16)
        copy = pltpu.make_async_copy(new.at[rows], new_h.at[rows], sems.at[3 + f])
        copy.start()
        copies.append(copy)
    for c in copies:
        c.wait()


def shards(atmos_state, horiz_wind, route_map, diffusivity, branch_mask, phys_state):
    q = atmos_state.reshape(ALL_ROWS, YD)
    wind = horiz_wind.reshape(2, ROWS, YD)
    const = jnp.asarray(constants())
    hbm = pl.BlockSpec(memory_space=pltpu.HBM)
    whole = pl.BlockSpec(memory_space=pltpu.VMEM)
    top = TOP * ROWS
    state = pl.pallas_call(
        exchange_kernel,
        out_shape=(
            pltpu.VMEM((COLS, 2, CAP, LEV), BF16),
            pltpu.VMEM((SLOTS, ROWS), BF16),
            pltpu.VMEM((top, YD), F32),
            pltpu.VMEM((XD, LEV, YD), F32),
            pltpu.VMEM((ALL_ROWS - top, YD), BF16),
            pltpu.VMEM((PF, LEV, SLOTS), F32),
        ),
        in_specs=[hbm] * 7,
        out_specs=(whole,) * 6,
        scratch_shapes=[
            pltpu.VMEM((ALL_ROWS, YD), BF16),
            pltpu.VMEM((XD, YD), jnp.int32),
            pltpu.VMEM((LEV, SLOTS), F32),
            pltpu.VMEM((LEV, SLOTS), jnp.int32),
            pltpu.VMEM((2, ROWS, YD), F32),
            pltpu.VMEM((384, 256), BF16),
            pltpu.VMEM((SLOTS, LEV), F32),
            pltpu.VMEM((2, LEV, SLOTS), F32),
            pltpu.SemaphoreType.DMA((8,)),
            pltpu.VMEM((COLS, 2, CAP, LEV), BF16),
            pltpu.VMEM((COLS, 2, CAP, LEV), BF16),
            pltpu.VMEM((COLS, 2, CAP, LEV), BF16),
            pltpu.VMEM((ALL_ROWS, YD), F32),
            pltpu.VMEM((FIELDS, XD, LEV, YD), BF16),
            pltpu.VMEM((ALL_ROWS, YD), F32),
            pltpu.VMEM((2, FIELDS, LEV, YD), BF16),
            pltpu.VMEM((2 * YPAD, ROWS), BF16),
            pltpu.VMEM((2 * YPAD, ROWS), BF16),
            pltpu.VMEM((2, XD, LEV, YD), F32),
            pltpu.VMEM((XD * LEV, YD), F32),
            pltpu.VMEM((ROWS, YD), F32),
            pltpu.VMEM((8 * LEV, 128), F32),
            pltpu.VMEM((8 * LEV, 128), F32),
            pltpu.SemaphoreType.DMA((2,)),
            pltpu.SemaphoreType.DMA((2,)),
            pltpu.SemaphoreType.DMA((4,)),
            pltpu.SemaphoreType.DMA((4,)),
        ],
        compiler_params=pltpu.CompilerParams(
            collective_id=0, has_side_effects=True, vmem_limit_bytes=54 << 20
        ),
    )(q, route_map, diffusivity, branch_mask, phys_state, wind, const)
    new, phys_next = pl.pallas_call(
        update_kernel,
        out_shape=(
            jax.ShapeDtypeStruct((ALL_ROWS, YD), BF16),
            jax.ShapeDtypeStruct((PF, LEV, SLOTS), F32),
        ),
        in_specs=[whole] * 6,
        out_specs=(hbm,) * 2,
        scratch_shapes=[
            pltpu.VMEM((top, YD), F32),
            pltpu.VMEM((top, YD), BF16),
            pltpu.SemaphoreType.DMA((3 + TOP,)),
        ],
        compiler_params=pltpu.CompilerParams(vmem_limit_bytes=32 << 20),
    )(*state)
    return new.reshape(FIELDS, LEV, XD, YD), phys_next


def solution(mesh):
    return jax.shard_map(
        shards,
        mesh=mesh,
        in_specs=(
            P(None, None, "edge", "cols"),
            P(None, None, "edge", "cols"),
            P("edge", "cols"),
            P(None, ("edge", "cols")),
            P(None, ("edge", "cols")),
            P(None, None, ("edge", "cols")),
        ),
        out_specs=(P(None, None, "edge", "cols"), P(None, None, ("edge", "cols"))),
        check_vma=False,
    )
```

```python
import functools

import jax
import jax.numpy as jnp
import numpy as np
from jax import lax
from jax.experimental import pallas as pl
from jax.experimental.pallas import tpu as pltpu
from jax.sharding import PartitionSpec as P

MESH = pl.DeviceIdType.MESH
F32, BF16 = jnp.float32, jnp.bfloat16
FIELDS, LEV, XD, YD = 11, 128, 4, 128
EDGE, COLS, CAP, PF = 4, 32, 32, 8
SLOTS = COLS * CAP
ROWS = LEV * XD
ALL_ROWS = FIELDS * ROWS
TOP = 4
YPAD = 16
PENALTY = 3.0
STEP_SIZE = 0.05
LATENT_WARM = 0.5
LATENT_ICE = 0.6
COUPLE_WARM = [0.8, -0.6, 0.5, 0.9, -0.7, 0.4, 1.0, -0.5]
COUPLE_ICE = [-0.4, 0.7, 0.9, -0.5, 0.6, -0.8, 0.3, 0.7]


def gll_matrix():
    nodes = np.array([-1.0, -1.0 / np.sqrt(5.0), 1.0 / np.sqrt(5.0), 1.0])
    prod = [np.prod([nodes[i] - nodes[j] for j in range(4) if j != i]) for i in range(4)]
    table = np.zeros((4, 4))
    for i in range(4):
        for j in range(4):
            if i != j:
                table[i, j] = prod[i] / (prod[j] * (nodes[i] - nodes[j]))
            else:
                table[i, i] = sum(1.0 / (nodes[i] - nodes[k]) for k in range(4) if k != i)
    return table


def split_bf16(table):
    high = table.astype(np.float32).astype(BF16)
    low = (table - high.astype(np.float64)).astype(np.float32).astype(BF16)
    return high, low


def derivative():
    own = gll_matrix()
    own[0, 0] += PENALTY
    own[3, 3] -= PENALTY
    return -STEP_SIZE * own


def constants():
    own = derivative() / -STEP_SIZE
    gy = np.zeros((YD, YD))
    for el in range(YD // 4):
        gy[4 * el : 4 * el + 4, 4 * el : 4 * el + 4] = own.T
        if el:
            gy[4 * el - 1, 4 * el] = -PENALTY
        if el < YD // 4 - 1:
            gy[4 * el + 4, 4 * el + 3] = PENALTY
    ey = np.zeros((YD, YD))
    ey[:YPAD, 0] = -PENALTY
    ey[YPAD : 2 * YPAD, YD - 1] = PENALTY
    table = np.concatenate(split_bf16(-STEP_SIZE * np.concatenate([gy, ey], 0)), 1)
    tri = np.triu(np.ones((YD, YD)), 1)
    square = np.concatenate([tri, np.eye(128)], 1).astype(BF16)
    return np.concatenate([table, square], 0)


def far_first():
    def dist(k):
        z, y = k // 8, (k // 2) % 4
        return min(z, 4 - z) + min(y, 4 - y)

    return sorted(range(1, COLS), key=lambda k: -dist(k))


def softplus(x):
    return jnp.maximum(x, 0.0) + jnp.log1p(jnp.exp(-jnp.abs(x)))


def rates(phys0, phys1, mask):
    warm = jnp.where((mask & 1) == 1, softplus(phys0), 0.0)
    ice = jnp.where(mask >= 2, softplus(phys1), 0.0)
    return warm, ice


def dot(a, b):
    return jnp.dot(a, b, preferred_element_type=F32)


def dot_t(a, b):
    return lax.dot_general(a, b, (((1,), (1,)), ((), ())), preferred_element_type=F32)


def t_dot(a, b):
    return lax.dot_general(a, b, (((0,), (0,)), ((), ())), preferred_element_type=F32)


def exchange_kernel(
    q_h, route_h, kv_h, mask_h, phys_h, wind_h, const_h,
    recv_b, hot, pre, vap, rest, phys,
    qv, route, kv, mask, wind, const, group, gain, in_sem,
    snd_a, snd_b, recv_a, sol, qp, tn, xr, ys, yr, wp, par, cu, gkv, gcu,
    ss, rs, hss, hrs,
):
    e, me = lax.axis_index("edge"), lax.axis_index("cols")
    core, yy, zz = me % 2, (me // 2) % 4, me // 8
    order = far_first()

    def peer(k):
        return ((zz + k // 8) % 4) * 8 + ((yy + (k // 2) % 4) % 4) * 2 + (core + k % 2) % 2

    up_x, down_x = (e + 1) % EDGE, (e + EDGE - 1) % EDGE
    up_y, down_y = (me + 1) % COLS, (me + COLS - 1) % COLS
    loads = [
        pltpu.make_async_copy(a, b, in_sem.at[i])
        for i, (a, b) in enumerate(
            (
                (const_h, const), (kv_h, kv), (route_h, route), (q_h, qv),
                (mask_h, mask), (phys_h.at[pl.ds(0, 2)], phys.at[pl.ds(0, 2)]), (wind_h, wind),
                (phys_h.at[pl.ds(2, PF - 2)], phys.at[pl.ds(2, PF - 2)]),
            )
        )
    ]
    for c in loads[:4]:
        c.start()
    bar = pltpu.get_barrier_semaphore()
    for k in order[::-1]:
        pl.semaphore_signal(bar, inc=1, device_id=(e, peer(k)), device_id_type=MESH)
    for to in (up_x, down_x):
        pl.semaphore_signal(bar, inc=1, device_id=(to, me), device_id_type=MESH)
    tri = const.at[pl.ds(256, 128), pl.ds(0, 128)]
    eye = const.at[pl.ds(256, 128), pl.ds(128, 128)]

    def turn(j, value):
        turned = dot_t(eye[...], value.astype(BF16)).astype(BF16)
        return turned.reshape(4, CAP, LEV)

    loads[0].wait()
    loads[1].wait()
    for c in loads[4:7]:
        c.start()
    for j in range(8):
        coupling = kv[:, j * 128 : (j + 1) * 128]
        snd_a[4 * j : 4 * j + 4, 0] = turn(j, coupling)
        gkv[pl.ds(j, LEV, stride=8), :] = coupling

    loads[2].wait()
    dest_at = lax.broadcasted_iota(jnp.int32, (COLS, YD), 0)
    slot_at = lax.broadcasted_iota(jnp.int32, (SLOTS, YD), 0)
    before = jnp.zeros((COLS, 1), F32)
    for x in range(XD):
        chosen = dest_at == route[x : x + 1, :]
        chosen_f = jnp.where(chosen, 1.0, 0.0)
        earlier = dot(chosen_f.astype(BF16), tri[...]) + before
        before = before + jnp.sum(chosen_f, axis=1, keepdims=True)
        rank = jnp.sum(jnp.where(chosen, earlier, 0.0), axis=0, keepdims=True)
        slots = route[x : x + 1, :] * CAP + rank.astype(jnp.int32)
        hot[:, x * YD : (x + 1) * YD] = jnp.where(slot_at == slots, 1.0, 0.0).astype(BF16)

    loads[3].wait()

    def planes(f, carry):
        rows = pl.ds(pl.multiple_of(f * ROWS, ROWS), ROWS)
        sol[rows, :] = qv[rows, :].astype(F32)
        for x in range(XD):
            qp[f, x] = sol[pl.ds(f * ROWS + x, LEV, stride=XD), :].astype(BF16)
        return carry

    lax.fori_loop(0, FIELDS, planes, 0)
    total = dot_t(hot[...], jnp.concatenate([qp[1, x] for x in range(XD)], axis=1))
    snd_a[:, 1] = total.astype(BF16).reshape(COLS, CAP, LEV)

    fields = jnp.concatenate([qp[f].reshape(ROWS, YD) for f in range(FIELDS)], axis=1)
    at = lax.broadcasted_iota(jnp.int32, (YD, YD), 0)
    lane = lax.broadcasted_iota(jnp.int32, (YD, YD), 1)
    pick = [
        jnp.where(((at == 0) & (lane == f)) | ((at == YD - 1) & (lane == YPAD + f)), 1.0, 0.0)
        for f in range(FIELDS)
    ]
    ends = dot(fields, jnp.concatenate(pick, axis=0).astype(BF16)).astype(BF16)
    ys[...] = dot_t(eye[0 : 2 * YPAD, :], ends).astype(BF16)

    pl.semaphore_wait(bar, COLS - 1 + 2)
    y_copies, x_copies = [], []
    for i, to in ((0, down_y), (1, up_y)):
        y_copies.append(
            pltpu.make_async_remote_copy(
                ys.at[pl.ds(i * YPAD, YPAD)], yr.at[pl.ds((1 - i) * YPAD, YPAD)],
                hss.at[2 + i], hrs.at[3 - i],
                device_id=(e, to), device_id_type=MESH,
            )
        )
    for i, to in ((0, down_x), (1, up_x)):
        x_copies.append(
            pltpu.make_async_remote_copy(
                qp.at[:, i * (XD - 1)], xr.at[1 - i], hss.at[i], hrs.at[1 - i],
                device_id=(to, me), device_id_type=MESH,
            )
        )
    for c in y_copies + x_copies:
        c.start()

    def message(k, part):
        to = peer(k)
        source, target = ((snd_a, recv_a), (snd_b, recv_b))[part]
        return pltpu.make_async_remote_copy(
            source.at[to], target.at[me], ss.at[part], rs.at[part],
            device_id=(e, to), device_id_type=MESH,
        )

    def settle(part):
        source, target = ((snd_a, recv_a), (snd_b, recv_b))[part]
        others = pl.ds(0, COLS - 1)
        pltpu.make_async_remote_copy(
            source.at[others], target.at[others], ss.at[part], rs.at[part],
            device_id=(e, peer(1)), device_id_type=MESH,
        ).wait()

    for k in order:
        message(k, 0).start()
    loads[4].wait()
    loads[5].wait()
    for j in range(8):
        lanes = slice(j * 128, (j + 1) * 128)
        warm, ice = rates(phys[0, :, lanes], phys[1, :, lanes], mask[:, lanes])
        inv = 1.0 / (1.0 + warm + ice)
        share = inv + inv * inv
        gain[0, :, lanes] = warm * share
        gain[1, :, lanes] = ice * share
        snd_b[4 * j : 4 * j + 4, 0] = turn(j, warm)
        snd_b[4 * j : 4 * j + 4, 1] = turn(j, ice)
    loads[7].start()
    recv_a[pl.ds(me, 1)] = snd_a[pl.ds(me, 1)]
    recv_b[pl.ds(me, 1)] = snd_b[pl.ds(me, 1)]

    loads[6].wait()
    for i in range(2):
        for x in range(XD):
            wp[i, x] = wind[i, pl.ds(x, LEV, stride=XD), :]
    for c in y_copies:
        c.wait()
    y_halo = t_dot(yr[...], eye[0 : 2 * YPAD, :])
    wide = lax.broadcasted_iota(jnp.int32, (ROWS, YD), 1)
    along = derivative()

    def dynamics(f, carry):
        near = jnp.where((wide == f) | (wide == YPAD + f), y_halo, 0.0).astype(BF16)
        both = jnp.concatenate([qp[f].reshape(ROWS, YD), near], axis=1)
        dy = dot(both, const[0:256, :])
        own = [qp[f, x].astype(F32) for x in range(XD)]
        for x in range(XD):
            dx = sum(float(along[x, i]) * own[i] for i in range(XD) if abs(along[x, i]) > 1e-9)
            rows = slice(x * LEV, (x + 1) * LEV)
            tn[pl.ds(f * ROWS + x, LEV, stride=XD), :] = wp[0, x] * dx + wp[1, x] * (
                dy[rows, :YD] + dy[rows, YD:]
            )
        return carry

    lax.fori_loop(0, FIELDS, dynamics, 0)
    for k in order:
        message(k, 1).start()

    settle(0)
    here = t_dot(recv_a[:, 0].reshape(SLOTS, LEV), hot[...])
    for x in range(XD):
        par[x * LEV : (x + 1) * LEV, :] = here[:, x * YD : (x + 1) * YD]
    for j in range(8):
        vapour = recv_a[4 * j : 4 * j + 4, 1].reshape(128, LEV)
        group[pl.ds(j, LEV, stride=8), :] = dot_t(eye[...], vapour)
    solve(sol, par, cu, group, gkv, gcu)

    loads[7].wait()
    couple(phys, gain, group)
    for c in x_copies:
        c.wait()

    def corrections(f, carry):
        for i, x, sign in ((0, 0, 1.0), (1, XD - 1, -1.0)):
            rows = pl.ds(f * ROWS + x, LEV, stride=XD)
            tn[rows, :] += (sign * STEP_SIZE * PENALTY) * wp[0, x] * xr[i, f].astype(F32)
        return carry

    lax.fori_loop(0, FIELDS, corrections, 0)
    top = TOP * ROWS
    pre[...] = sol[:top, :] + tn[:top, :]
    for x in range(XD):
        vap[x] = sol[pl.ds(ROWS + x, LEV, stride=XD), :]
    rest[...] = (sol[top:, :] + tn[top:, :]).astype(BF16)
    settle(1)


def solve(sol, par, cu, group, gkv, gcu):
    def forward(k, carry):
        kv_t, cu_t, kv_g, cu_g, prev, prev_g = carry
        here = par[pl.ds(k, XD, stride=LEV), :]
        inv = 1.0 / (1.0 + here + kv_t - kv_t * cu_t)
        low = kv_t * inv
        cu_t = here * inv
        at = pl.multiple_of(k * XD, XD)
        cu[pl.ds(at, XD), :] = cu_t
        values = []
        for f in range(FIELDS):
            rows = pl.ds(f * ROWS + at, XD)
            value = sol[rows, :] * inv + low * prev[f]
            sol[rows, :] = value
            values.append(value)
        at8 = pl.ds(pl.multiple_of(k * 8, 8), 8)
        here_g = gkv[at8, :]
        inv_g = 1.0 / (1.0 + here_g + kv_g - kv_g * cu_g)
        low_g = kv_g * inv_g
        cu_g = here_g * inv_g
        gcu[at8, :] = cu_g
        value_g = group[at8, :] * inv_g + low_g * prev_g
        group[at8, :] = value_g
        return here, cu_t, here_g, cu_g, tuple(values), value_g

    zt, zg = jnp.zeros((XD, YD), F32), jnp.zeros((8, 128), F32)
    lax.fori_loop(0, LEV, forward, (zt, zt, zg, zg, (zt,) * FIELDS, zg), unroll=16)

    def backward(i, carry):
        after, after_g = carry
        k = LEV - 1 - i
        at = pl.multiple_of(k * XD, XD)
        cu_t = cu[pl.ds(at, XD), :]
        values = []
        for f in range(FIELDS):
            rows = pl.ds(f * ROWS + at, XD)
            value = sol[rows, :] + cu_t * after[f]
            sol[rows, :] = value
            values.append(value)
        at8 = pl.ds(pl.multiple_of(k * 8, 8), 8)
        value_g = group[at8, :] + gcu[at8, :] * after_g
        group[at8, :] = value_g
        return tuple(values), value_g

    lax.fori_loop(0, LEV, backward, ((zt,) * FIELDS, zg), unroll=16)


def couple(phys, gain, group):
    for j in range(8):
        lanes = slice(j * 128, (j + 1) * 128)
        vapour = group[pl.ds(j, LEV, stride=8), :]
        warm, ice = gain[0, :, lanes] * vapour, gain[1, :, lanes] * vapour
        for f in range(PF):
            phys[f, :, lanes] += COUPLE_WARM[f] * warm + COUPLE_ICE[f] * ice


def update_kernel(recv_b, hot, pre, vap, rest, phys, new_h, phys_h, fin, new, sems):
    top = TOP * ROWS
    copies = [
        pltpu.make_async_copy(rest, new_h.at[pl.ds(top, ALL_ROWS - top)], sems.at[0]),
        pltpu.make_async_copy(phys, phys_h, sems.at[2]),
    ]
    for c in copies:
        c.start()
    both = jnp.concatenate([recv_b[:, i].reshape(SLOTS, LEV) for i in range(2)], axis=1)
    both = t_dot(both, hot[...])
    for x in range(XD):
        warm, ice = both[:LEV, x * YD : (x + 1) * YD], both[LEV:, x * YD : (x + 1) * YD]
        inv = 1.0 / (1.0 + warm + ice)
        passes = vap[x] * (inv + inv * inv)
        warm, ice = warm * passes, ice * passes
        gains = (LATENT_WARM * warm + LATENT_ICE * ice, -(warm + ice), warm, ice)
        for f in range(TOP):
            rows = pl.ds(f * ROWS + x, LEV, stride=XD)
            fin[rows, :] = pre[rows, :] + gains[f]
    for f in range(TOP):
        rows = pl.ds(f * ROWS, ROWS)
        new[rows, :] = fin[rows, :].astype(BF16)
        copy = pltpu.make_async_copy(new.at[rows], new_h.at[rows], sems.at[3 + f])
        copy.start()
        copies.append(copy)
    for c in copies:
        c.wait()


def shards(atmos_state, horiz_wind, route_map, diffusivity, branch_mask, phys_state):
    q = atmos_state.reshape(ALL_ROWS, YD)
    wind = horiz_wind.reshape(2, ROWS, YD)
    const = jnp.asarray(constants())
    hbm = pl.BlockSpec(memory_space=pltpu.HBM)
    whole = pl.BlockSpec(memory_space=pltpu.VMEM)
    top = TOP * ROWS
    state = pl.pallas_call(
        exchange_kernel,
        out_shape=(
            pltpu.VMEM((COLS, 2, CAP, LEV), BF16),
            pltpu.VMEM((SLOTS, ROWS), BF16),
            pltpu.VMEM((top, YD), F32),
            pltpu.VMEM((XD, LEV, YD), F32),
            pltpu.VMEM((ALL_ROWS - top, YD), BF16),
            pltpu.VMEM((PF, LEV, SLOTS), F32),
        ),
        in_specs=[hbm] * 7,
        out_specs=(whole,) * 6,
        scratch_shapes=[
            pltpu.VMEM((ALL_ROWS, YD), BF16),
            pltpu.VMEM((XD, YD), jnp.int32),
            pltpu.VMEM((LEV, SLOTS), F32),
            pltpu.VMEM((LEV, SLOTS), jnp.int32),
            pltpu.VMEM((2, ROWS, YD), F32),
            pltpu.VMEM((384, 256), BF16),
            pltpu.VMEM((SLOTS, LEV), F32),
            pltpu.VMEM((2, LEV, SLOTS), F32),
            pltpu.SemaphoreType.DMA((8,)),
            pltpu.VMEM((COLS, 2, CAP, LEV), BF16),
            pltpu.VMEM((COLS, 2, CAP, LEV), BF16),
            pltpu.VMEM((COLS, 2, CAP, LEV), BF16),
            pltpu.VMEM((ALL_ROWS, YD), F32),
            pltpu.VMEM((FIELDS, XD, LEV, YD), BF16),
            pltpu.VMEM((ALL_ROWS, YD), F32),
            pltpu.VMEM((2, FIELDS, LEV, YD), BF16),
            pltpu.VMEM((2 * YPAD, ROWS), BF16),
            pltpu.VMEM((2 * YPAD, ROWS), BF16),
            pltpu.VMEM((2, XD, LEV, YD), F32),
            pltpu.VMEM((XD * LEV, YD), F32),
            pltpu.VMEM((ROWS, YD), F32),
            pltpu.VMEM((8 * LEV, 128), F32),
            pltpu.VMEM((8 * LEV, 128), F32),
            pltpu.SemaphoreType.DMA((2,)),
            pltpu.SemaphoreType.DMA((2,)),
            pltpu.SemaphoreType.DMA((4,)),
            pltpu.SemaphoreType.DMA((4,)),
        ],
        compiler_params=pltpu.CompilerParams(
            collective_id=0, has_side_effects=True, vmem_limit_bytes=54 << 20
        ),
    )(q, route_map, diffusivity, branch_mask, phys_state, wind, const)
    new, phys_next = pl.pallas_call(
        update_kernel,
        out_shape=(
            jax.ShapeDtypeStruct((ALL_ROWS, YD), BF16),
            jax.ShapeDtypeStruct((PF, LEV, SLOTS), F32),
        ),
        in_specs=[whole] * 6,
        out_specs=(hbm,) * 2,
        scratch_shapes=[
            pltpu.VMEM((top, YD), F32),
            pltpu.VMEM((top, YD), BF16),
            pltpu.SemaphoreType.DMA((3 + TOP,)),
        ],
        compiler_params=pltpu.CompilerParams(vmem_limit_bytes=32 << 20),
    )(*state)
    return new.reshape(FIELDS, LEV, XD, YD), phys_next


def solution(mesh):
    return jax.shard_map(
        shards,
        mesh=mesh,
        in_specs=(
            P(None, None, "edge", "cols"),
            P(None, None, "edge", "cols"),
            P("edge", "cols"),
            P(None, ("edge", "cols")),
            P(None, ("edge", "cols")),
            P(None, None, ("edge", "cols")),
        ),
        out_specs=(P(None, None, "edge", "cols"), P(None, None, ("edge", "cols"))),
        check_vma=False,
    )
```
